256 devices in a mesh: head: 4 (over x), expert: 64 (over y, z, core).
Axes of the slice: x: 4, y: 4, z: 8, core: 2. Of those that a mesh axis runs over, the one named last changes fastest.
Arguments:
- query_rows: bfloat16 [4, 256, 4096], P(None, 'expert', 'head'), may hold values from -0.59765625 to 0.59765625
- key_rows: bfloat16 [4, 256, 4096], P(None, 'expert', 'head'), may hold values from -6 to 6
- value_rows: bfloat16 [4, 256, 4096], P(None, 'expert', 'head'), may hold values from -6 to 6
- forget: float32 [32], P('head'), may hold values from 0.02 to 2
- head_state: bfloat16 [256, 32, 128, 128], P('expert', 'head'), may hold values from -6 to 6
- out_weight: bfloat16 [4096, 6144], P('head', 'expert'), may hold values from -0.09375 to 0.09375
- route_ids: int32 [4, 256, 2], P(None, 'expert'), may hold values from 0 to 15, as said below
- route_gate: float32 [4, 256, 2], P(None, 'expert'), may hold values from 0.1 to 0.9
- gate_weight: bfloat16 [64, 6144, 1152], P('expert', None, 'head'), may hold values from -0.078125 to 0.078125
- up_weight: bfloat16 [64, 6144, 1152], P('expert', None, 'head'), may hold values from -0.078125 to 0.078125
- down_weight: bfloat16 [64, 1152, 6144], P('expert', 'head'), may hold values from -0.09375 to 0.09375
Outputs:
- mixed: bfloat16 [4, 256, 6144], P(None, 'expert')
- moe_out: bfloat16 [4, 256, 6144], P(None, 'expert')
- state_out: bfloat16 [256, 32, 128, 128], P('expert', 'head')
The draws below stay inside these ranges and needn't reach their ends.
Inputs may be any that keep to these rules, and one draw needn't show every extreme that they name: `route_ids`: each row names two different experts. In each step at most 2 of the 4 rows of one device name the same expert, and one expert, drawn anew for each step, is named by exactly 2 rows of every device.
All inputs are finite; a program needn't handle non-finite values.
Results may differ from the reference program's by a relative error of at most 0.008.
Values may be sent and summed in bfloat16 or wider, within the bound.
No kernel may reach another device: no remote copies, remote signals or barrier semaphores. Data moves between devices by JAX's collectives and lax.ppermute only.
A program may use at most 128 MiB of HBM per device.

```python
import math
import jax
import jax.numpy as jnp
from jax import lax

D = 6144
HEADS = 32
DK = 128
FF = 4608
ROW_DEV = 4
STEPS = 4
ROWS = 256
EXPERTS = 16
SLICES = 4
CAP = 2
N_EXPERT = 64


def draw_route_ids(key, part):
    key = jax.random.fold_in(key, 11)
    subkeys = jax.random.split(key, 6)
    blocks = ROWS // ROW_DEV
    crowded = jax.random.randint(subkeys[0], (STEPS, 1), 0, EXPERTS).astype(jnp.int32)
    ranking = jax.random.permutation(subkeys[1], EXPERTS)
    weighting = jnp.where(ranking < max(1, EXPERTS // 4), 4, 1).astype(jnp.int32)
    raw_scores = jax.random.randint(subkeys[2], (STEPS, blocks, EXPERTS), 0, 1 << 16).astype(jnp.int32)
    labels = jnp.arange(EXPERTS, dtype=jnp.int32)
    scores = raw_scores * weighting * EXPERTS + labels
    scores = jnp.where(labels == crowded[:, :, None], -1, scores)
    picked = lax.top_k(scores, 4)[1].astype(jnp.int32)
    pick_one = picked[..., 0]
    pick_two = picked[..., 1]
    pick_three = picked[..., 2]
    pick_four = picked[..., 3]
    toggle = jax.random.randint(subkeys[3], (STEPS, blocks), 0, 2)
    final_pick = jnp.where((toggle == 1) & (EXPERTS >= 5), pick_four, pick_three)
    crowded_rows = jnp.broadcast_to(crowded, (STEPS, blocks))
    routed = jnp.stack([jnp.stack([crowded_rows, pick_one], -1), jnp.stack([crowded_rows, pick_two], -1), jnp.stack([pick_one, pick_three], -1), jnp.stack([pick_two, final_pick], -1)], axis=2)
    shuffle = jax.random.randint(subkeys[4], (STEPS, blocks, 4), 0, 1 << 16).astype(jnp.int32) * 4 + jnp.arange(4, dtype=jnp.int32)
    arrange = jnp.argsort(shuffle, axis=-1)
    routed = jnp.take_along_axis(routed, arrange[..., None], axis=2)
    flipped = jax.random.randint(subkeys[5], (STEPS, blocks, 4, 1), 0, 2)
    routed = jnp.where(flipped == 1, routed[..., ::-1], routed)
    return routed.reshape(STEPS, ROWS, 2).astype(jnp.int32)


def shard_levels(key, dims, cuts, smallest, largest):
    def one(position, shards_of):
        steps = jax.random.uniform(jax.random.fold_in(jax.random.fold_in(key, 6), position), (shards_of,), jnp.float32, smallest / len(cuts), largest / len(cuts))
        return jnp.repeat(jnp.exp(steps), dims[position] // shards_of).reshape((-1,) + (1,) * (len(dims) - position - 1))

    level = one(*cuts[0])
    for cut in cuts[1:]:
        level = level * one(*cut)
    return level


def centred(own_key, shape, deviation, limit, cuts=(), held_as=jnp.bfloat16):
    array = jax.random.normal(own_key, shape, jnp.float32) * deviation
    if len(cuts) > 0:
        array = shard_levels(own_key, shape, cuts, -0.22, 0.18) * array
    return jnp.clip(array, min=-limit, max=limit).astype(held_as)


def setup_inputs(seed: int = 0) -> dict:
    splits = jax.random.split(jax.random.key(seed), 12)
    return {
        "query_rows": centred(splits[0], (STEPS, ROWS, HEADS * DK), 0.09, 0.59765625, ((1, 64), (2, 4))),
        "key_rows": centred(splits[1], (STEPS, ROWS, HEADS * DK), 1.0, 6.0, ((1, 64), (2, 4))),
        "value_rows": centred(splits[2], (STEPS, ROWS, HEADS * DK), 1.0, 6.0, ((1, 64), (2, 4))),
        "forget": jnp.clip(jnp.exp(math.log(2.0) - 4.6051702 * jax.random.uniform(splits[3], (HEADS,), jnp.float32) ** shard_levels(splits[3], (HEADS,), ((0, 4),), -0.2, 0.2)), 0.02, 2.0),
        "head_state": centred(splits[4], (ROWS, HEADS, DK, DK), 1.0, 6.0, ((0, 64), (1, 4))),
        "out_weight": centred(splits[5], (HEADS * DK, D), (HEADS * DK) ** -0.5, 0.09375, ((0, 4), (1, 64))),
        "route_ids": draw_route_ids(jax.random.fold_in(splits[11], 71), 0),
        "route_gate": jnp.clip(0.1 + 0.79999997 * jax.random.uniform(splits[7], (STEPS, ROWS, 2), jnp.float32) ** shard_levels(splits[7], (STEPS, ROWS, 2), ((1, 64),), -0.2, 0.2), 0.1, 0.9),
        "gate_weight": centred(splits[8], (N_EXPERT, D, FF // SLICES), D ** -0.5, 0.078125, ((0, 64), (2, 4))),
        "up_weight": centred(splits[9], (N_EXPERT, D, FF // SLICES), D ** -0.5, 0.078125, ((0, 64), (2, 4))),
        "down_weight": centred(splits[10], (N_EXPERT, FF // SLICES, D), FF ** -0.5, 0.09375, ((0, 64), (1, 4))),
    }


def reference(query_rows, key_rows, value_rows, forget, head_state, out_weight, route_ids, route_gate, gate_weight, up_weight, down_weight):
    highest = lax.Precision.HIGHEST
    head_width = HEADS * DK
    split_shape = (STEPS, ROWS, HEADS, DK)
    query_float = query_rows.astype(jnp.float32).reshape(split_shape)
    key_float = key_rows.astype(jnp.float32).reshape(split_shape)
    value_float = value_rows.astype(jnp.float32).reshape(split_shape)
    decay_rate = jnp.exp(-forget)[None, :, None, None]
    carried = head_state.astype(jnp.float32)
    mixed_list = []
    for step_index in range(STEPS):
        carried = decay_rate * carried + jnp.einsum("rhi,rhj->rhij", key_float[step_index], value_float[step_index], precision=highest)
        attended = jnp.einsum("rhi,rhij->rhj", query_float[step_index], carried, precision=highest)
        attended = attended.astype(jnp.bfloat16).reshape(ROWS, head_width)
        mixed_list.append(jnp.dot(attended, out_weight, preferred_element_type=jnp.float32).astype(jnp.bfloat16))
    mixed_all = jnp.stack(mixed_list)
    state_out = carried.astype(jnp.bfloat16)

    piece_width = FF // SLICES
    gate_slabs = gate_weight.reshape(EXPERTS, SLICES, D, piece_width)
    up_slabs = up_weight.reshape(EXPERTS, SLICES, D, piece_width)
    down_slabs = down_weight.reshape(EXPERTS, SLICES, piece_width, D)
    slot_count = N_EXPERT * CAP
    onehot = (route_ids[..., None] == jnp.arange(EXPERTS, dtype=jnp.int32)).astype(jnp.int32)
    ranked = (jnp.cumsum(onehot.reshape(STEPS, ROWS * 2, EXPERTS), axis=1) - 1).reshape(STEPS, ROWS, 2, EXPERTS)
    landed = onehot[..., None] * (ranked[..., None] == jnp.arange(slot_count, dtype=jnp.int32)).astype(jnp.int32)
    placed = jnp.sum(landed, axis=2).astype(jnp.float32)
    weights = jnp.sum(landed.astype(jnp.float32) * route_gate[..., None, None], axis=2)
    mixed_float = mixed_all.astype(jnp.float32)

    def add_expert(total, expert_index):
        place_one = lax.dynamic_index_in_dim(placed, expert_index, 2, keepdims=False)
        weight_one = lax.dynamic_index_in_dim(weights, expert_index, 2, keepdims=False)
        gate_one = lax.dynamic_index_in_dim(gate_slabs, expert_index, 0, keepdims=False).astype(jnp.float32)
        up_one = lax.dynamic_index_in_dim(up_slabs, expert_index, 0, keepdims=False).astype(jnp.float32)
        down_one = lax.dynamic_index_in_dim(down_slabs, expert_index, 0, keepdims=False).astype(jnp.float32)
        gathered = jnp.einsum("trc,trd->tcd", place_one, mixed_float, precision=highest).astype(jnp.bfloat16)
        flat_rows = gathered.reshape(STEPS * slot_count, D).astype(jnp.float32)
        gated = jnp.einsum("nd,sdf->nsf", flat_rows, gate_one, precision=highest)
        lifted = jnp.einsum("nd,sdf->nsf", flat_rows, up_one, precision=highest)
        hidden = (jax.nn.silu(gated) * lifted).astype(jnp.bfloat16).astype(jnp.float32)
        output_rows = jnp.einsum("nsf,sfd->nd", hidden, down_one, precision=highest).reshape(STEPS, slot_count, D)
        return total + jnp.einsum("trc,tcd->trd", weight_one, output_rows, precision=highest), None

    total, unused = lax.scan(add_expert, jnp.zeros((STEPS, ROWS, D), jnp.float32), jnp.arange(EXPERTS, dtype=jnp.int32))
    return mixed_all, total.astype(jnp.bfloat16), state_out
```

```python
import jax
import jax.numpy as jnp
from jax import lax
from jax.sharding import Mesh, PartitionSpec as P

BLOCKS = ("y", "zp")
EXPERT = ("y", "zp", "zl", "core")
BF16 = jnp.bfloat16
F32 = jnp.float32
EXACT = lax.Precision.HIGHEST


def shift(array, axis, distance):
    size = lax.axis_size(axis)
    pairs = [(i, (i + distance) % size) for i in range(size)]
    return lax.ppermute(array, axis, pairs)


def spread(array, axis):
    size = lax.axis_size(axis)
    copies = jnp.broadcast_to(array[None], (size,) + array.shape)
    return lax.all_to_all(copies, axis, split_axis=0, concat_axis=0, tiled=True)


def attention(query_rows, key_rows, value_rows, forget, head_state):
    steps, rows, width = query_rows.shape
    heads = forget.shape[0]
    size = width // heads
    shape = (steps, rows, heads, size)
    query, key, value = (a.reshape(shape) for a in (query_rows, key_rows, value_rows))
    times = jnp.arange(steps, dtype=F32)
    power = jnp.exp(-forget[None, :] * jnp.arange(steps + 1, dtype=F32)[:, None])
    lag = times[:, None] - times[None, :]
    causal = jnp.where(
        lag[..., None] >= 0, jnp.exp(-forget * jnp.maximum(lag, 0.0)[..., None]), 0.0
    )
    from_state = jnp.einsum("trhi,rhij->trhj", query, head_state, preferred_element_type=F32)
    scores = jnp.einsum("trhi,srhi->tsrh", query, key, preferred_element_type=F32)
    scores = scores * causal[:, :, None, :]
    value_float = value.astype(F32)
    from_steps = sum(scores[:, s, :, :, None] * value_float[s][None] for s in range(steps))
    attended = power[1:, None, :, None] * from_state + from_steps
    attended = attended.astype(BF16).reshape(steps * rows, width)
    scaled_key = key.astype(F32) * power[steps - 1 :: -1][:steps, None, :, None]
    state = power[steps][None, :, None, None] * head_state.astype(F32) + jnp.einsum(
        "trhi,trhj->rhij", scaled_key, value_float, precision=EXACT
    )
    return attended, state.astype(BF16)


def place(ids, experts, capacity):
    rows = ids.shape[-2]
    flat = ids.reshape(ids.shape[:-2] + (rows * 2,))
    onehot = (flat[..., None] == jnp.arange(experts, dtype=jnp.int32)).astype(jnp.int32)
    ranked = jnp.cumsum(onehot, axis=-2) - 1
    landed = onehot[..., None] * (
        ranked[..., None] == jnp.arange(capacity, dtype=jnp.int32)
    ).astype(jnp.int32)
    landed = jnp.moveaxis(landed, (-2, -1), (0, 1)).astype(F32)
    return landed.reshape(landed.shape[:-1] + (rows, 2))


def gather_block(own):
    across = shift(own, "zl", 1)
    left, right, far = shift(own, "head", 1), shift(own, "head", -1), shift(own, "head", 2)
    across_left, across_right = shift(across, "head", 1), shift(across, "head", -1)
    across_far = shift(far, "zl", 1)
    return [own, left, right, far, across, across_left, across_right, across_far]


def scatter_block(parts):
    own, left, right, far, across, across_left, across_right, across_far = parts

    def add(*terms):
        return sum(t.astype(F32) for t in terms)

    from_right = shift(across_left, "head", -1)
    from_left = shift(across_right, "head", 1)
    from_far = shift(across_far, "zl", 1)
    got_left = shift(right, "head", 1)
    got_right = shift(left, "head", -1)
    got_far = shift(add(far, from_far).astype(BF16), "head", 2)
    got_across = shift(add(across, from_right, from_left).astype(BF16), "zl", 1)
    return add(own, got_left, got_right, got_far, got_across).astype(BF16)


def expert_ffn(rows, weights):
    total = 0.0
    for gate, up, down in weights:
        gated = jnp.dot(rows, gate, preferred_element_type=F32)
        lifted = jnp.dot(rows, up, preferred_element_type=F32)
        hidden = (jax.nn.silu(gated) * lifted).astype(BF16)
        total = total + jnp.dot(hidden, down, preferred_element_type=F32)
    return total.astype(BF16)


def shards(
    query_rows,
    key_rows,
    value_rows,
    forget,
    head_state,
    out_weight,
    route_ids,
    route_gate,
    gate_weight,
    up_weight,
    down_weight,
):
    steps, rows, _ = query_rows.shape
    blocks = lax.axis_size("y") * lax.axis_size("zp")
    experts = blocks
    capacity = rows // 2
    head = lax.axis_index("head")

    own_weights = (gate_weight[0], up_weight[0], down_weight[0])
    other_weights = tuple(shift(w, "core", 1) for w in own_weights)
    columns = lax.all_gather(out_weight, ("zl", "core"), axis=1, tiled=True)
    width = columns.shape[1]
    features = width * blocks

    own_ids = lax.dynamic_index_in_dim(route_ids, head, 0, keepdims=False)
    own_gate = lax.dynamic_index_in_dim(route_gate, head, 0, keepdims=False)
    peer_ids = lax.all_gather(own_ids, BLOCKS, axis=0, tiled=False)

    attended, state_out = attention(query_rows, key_rows, value_rows, forget, head_state)

    peers = spread(attended, BLOCKS).reshape(blocks, steps, rows, -1)
    peers = jnp.transpose(peers, (1, 2, 0, 3)).reshape(steps * rows * blocks, -1)
    partial = jnp.dot(peers, columns, preferred_element_type=F32)
    partial = partial.reshape(steps, rows * blocks, width)
    projected = lax.dynamic_index_in_dim(partial, head, 0, keepdims=False)
    for distance in range(1, steps):
        there = lax.rem(head + distance, steps)
        projected = projected + shift(
            lax.dynamic_index_in_dim(partial, there, 0, keepdims=False), "head", distance
        )
    projected = projected.astype(BF16).reshape(rows, blocks, width)

    returned = lax.all_to_all(
        jnp.transpose(projected, (1, 0, 2)), BLOCKS, split_axis=0, concat_axis=0, tiled=True
    )
    mixed = spread(jnp.transpose(returned, (1, 0, 2)).reshape(rows, features), "head")

    placed = jnp.sum(place(peer_ids, experts, capacity), axis=-1)
    packed = sum(
        placed[:, :, :, r, None] * projected[r].astype(F32)[None, None] for r in range(rows)
    ).astype(BF16)
    packed = lax.all_to_all(packed, BLOCKS, split_axis=0, concat_axis=0, tiled=True)
    piece = jnp.transpose(packed, (1, 2, 0, 3)).reshape(capacity * blocks, features)

    pieces = gather_block(piece)
    count = len(pieces)
    result = expert_ffn(jnp.concatenate(pieces, axis=0), (own_weights, other_weights))
    result = scatter_block(list(result.reshape(count, capacity * blocks, features)))

    result = jnp.transpose(result.reshape(capacity, blocks, features), (1, 0, 2))
    result = lax.all_to_all(result, BLOCKS, split_axis=0, concat_axis=0, tiled=True)
    weights = jnp.sum(place(own_ids, experts, capacity) * own_gate, axis=-1)
    combined = jnp.einsum(
        "esr,esd->rd", weights, result.astype(F32), precision=EXACT
    ).astype(BF16)
    moe_out = spread(combined, "head")
    return mixed, moe_out, state_out


def solution(mesh):
    shape = dict(mesh.shape)
    heads, peers = shape["head"], shape["expert"]
    split = (4, peers // 16, 2, 2)
    fine = Mesh(mesh.devices.reshape((heads,) + split), ("head",) + EXPERT)
    return jax.shard_map(
        shards,
        mesh=fine,
        in_specs=(
            P(None, EXPERT, "head"),
            P(None, EXPERT, "head"),
            P(None, EXPERT, "head"),
            P("head"),
            P(EXPERT, "head", None, None),
            P("head", EXPERT),
            P(None, EXPERT, None),
            P(None, EXPERT, None),
            P(EXPERT, None, "head"),
            P(EXPERT, None, "head"),
            P(EXPERT, "head", None),
        ),
        out_specs=(
            P(None, EXPERT, None),
            P(None, EXPERT, None),
            P(EXPERT, "head", None, None),
        ),
        check_vma=False,
    )
```

```python
import functools

import jax
import jax.numpy as jnp
from jax import lax
from jax.experimental import pallas as pl
from jax.experimental.pallas import tpu as pltpu
from jax.sharding import Mesh, PartitionSpec as P

BLOCKS = ("y", "zp")
EXPERT = ("y", "zp", "zl", "core")
BF16 = jnp.bfloat16
F32 = jnp.float32
LANES = 128
EXACT = lax.Precision.HIGHEST


def shift(array, axis, distance):
    size = lax.axis_size(axis)
    pairs = [(i, (i + distance) % size) for i in range(size)]
    return lax.ppermute(array, axis, pairs)


def spread(array, axis):
    size = lax.axis_size(axis)
    copies = jnp.broadcast_to(array[None], (size,) + array.shape)
    return lax.all_to_all(copies, axis, split_axis=0, concat_axis=0, tiled=True)


def attention(query_rows, key_rows, value_rows, forget, head_state):
    steps, rows, width = query_rows.shape
    heads = forget.shape[0]
    size = width // heads
    shape = (steps, rows, heads, size)
    query, key, value = (a.reshape(shape) for a in (query_rows, key_rows, value_rows))
    times = jnp.arange(steps, dtype=F32)
    power = jnp.exp(-forget[None, :] * jnp.arange(steps + 1, dtype=F32)[:, None])
    lag = times[:, None] - times[None, :]
    causal = jnp.where(
        lag[..., None] >= 0, jnp.exp(-forget * jnp.maximum(lag, 0.0)[..., None]), 0.0
    )
    from_state = jnp.einsum("trhi,rhij->trhj", query, head_state, preferred_element_type=F32)
    scores = jnp.einsum("trhi,srhi->tsrh", query, key, preferred_element_type=F32)
    scores = scores * causal[:, :, None, :]
    value_float = value.astype(F32)
    from_steps = sum(scores[:, s, :, :, None] * value_float[s][None] for s in range(steps))
    attended = power[1:, None, :, None] * from_state + from_steps
    attended = attended.astype(BF16).reshape(steps * rows, width)
    scaled_key = key.astype(F32) * power[steps - 1 :: -1][:steps, None, :, None]
    state = power[steps][None, :, None, None] * head_state.astype(F32) + jnp.einsum(
        "trhi,trhj->rhij", scaled_key, value_float, precision=EXACT
    )
    return attended, state.astype(BF16)


def place(ids, experts, capacity):
    rows = ids.shape[-2]
    flat = ids.reshape(ids.shape[:-2] + (rows * 2,))
    onehot = (flat[..., None] == jnp.arange(experts, dtype=jnp.int32)).astype(jnp.int32)
    ranked = jnp.cumsum(onehot, axis=-2) - 1
    landed = onehot[..., None] * (
        ranked[..., None] == jnp.arange(capacity, dtype=jnp.int32)
    ).astype(jnp.int32)
    landed = jnp.moveaxis(landed, (-2, -1), (0, 1)).astype(F32)
    return landed.reshape(landed.shape[:-1] + (rows, 2))


def gather_block(own):
    half = own.shape[0] // 2
    left, right, across = shift(own, "head", 1), shift(own, "head", -1), shift(own, "zl", 1)

    def halves(one, other):
        return jnp.concatenate([one, other], axis=0)

    by_left = shift(halves(left[:half], across[:half]), "head", 1)
    by_right = shift(halves(right[half:], across[half:]), "head", -1)
    by_across = shift(halves(left[half:], right[:half]), "zl", 1)
    last_left = shift(by_left[half:], "head", 1)
    last_right = shift(by_right[half:], "head", -1)
    return [own, left, right, across, by_left, by_right, by_across, last_left, last_right]


def scatter_block(parts):
    own, left, right, across, by_left, by_right, by_across, last_left, last_right = parts
    half = own.shape[0] // 2

    def add(*terms):
        return sum(t.astype(F32) for t in terms).astype(BF16)

    def halves(one, other):
        return jnp.concatenate([one, other], axis=0)

    from_right = shift(last_left, "head", -1)
    from_left = shift(last_right, "head", 1)
    by_left = halves(by_left[:half], add(by_left[half:], from_right))
    by_right = halves(by_right[:half], add(by_right[half:], from_left))
    from_right = shift(by_left, "head", -1)
    from_left = shift(by_right, "head", 1)
    from_across = shift(by_across, "zl", 1)
    left = add(left, halves(from_right[:half], from_across[:half]))
    right = add(right, halves(from_across[half:], from_left[:half]))
    across = add(across, halves(from_right[half:], from_left[half:]))
    return add(own, shift(left, "head", -1), shift(right, "head", 1), shift(across, "zl", 1))


def ffn_kernel(count, inner, *refs):
    rows, refs = refs[:count], refs[count:]
    gate, up, down = refs[0:2], refs[2:4], refs[4:6]
    outs, refs = refs[6 : 6 + count], refs[6 + count :]
    gated, lifted, hidden = refs
    step = pl.program_id(0)

    @pl.when(step == 0)
    def _():
        gated[...] = jnp.zeros_like(gated)
        lifted[...] = jnp.zeros_like(lifted)

    @pl.when(step < inner)
    def _():
        block = jnp.concatenate([r[...] for r in rows], axis=0)
        for i in range(2):
            gated[i] += jnp.dot(block, gate[i][...], preferred_element_type=F32)
            lifted[i] += jnp.dot(block, up[i][...], preferred_element_type=F32)

    @pl.when(step == inner - 1)
    def _():
        value = gated[...]
        hidden[...] = (value / (1.0 + jnp.exp(-value)) * lifted[...]).astype(BF16)

    @pl.when(step >= inner)
    def _():
        total = jnp.dot(hidden[0], down[0][...], preferred_element_type=F32)
        total += jnp.dot(hidden[1], down[1][...], preferred_element_type=F32)
        total = total.astype(BF16)
        start = 0
        for out in outs:
            out[...] = total[start : start + out.shape[0]]
            start += out.shape[0]


def expert_ffn(parts, gate, up, down):
    features, width = gate[0].shape
    total_rows = sum(p.shape[0] for p in parts)
    tile = min(features, 1024)
    inner = features // tile

    def first(i):
        return jnp.minimum(i, inner - 1)

    def second(i):
        return jnp.maximum(i - inner, 0)

    return pl.pallas_call(
        functools.partial(ffn_kernel, len(parts), inner),
        grid=(2 * inner,),
        in_specs=[pl.BlockSpec((p.shape[0], tile), lambda i: (0, first(i))) for p in parts]
        + [pl.BlockSpec((tile, width), lambda i: (first(i), 0))] * 4
        + [pl.BlockSpec((width, tile), lambda i: (0, second(i)))] * 2,
        out_specs=[pl.BlockSpec((p.shape[0], tile), lambda i: (0, second(i))) for p in parts],
        out_shape=[jax.ShapeDtypeStruct(p.shape, BF16) for p in parts],
        scratch_shapes=[
            pltpu.VMEM((2, total_rows, width), F32),
            pltpu.VMEM((2, total_rows, width), F32),
            pltpu.VMEM((2, total_rows, width), BF16),
        ],
        compiler_params=pltpu.CompilerParams(vmem_limit_bytes=32 * 1024 * 1024),
        cost_estimate=pl.CostEstimate(
            flops=12 * total_rows * features * width,
            bytes_accessed=12 * features * width + 4 * total_rows * features,
            transcendentals=2 * total_rows * width,
        ),
    )(*parts, *gate, *up, *down)


def block_columns(out_weight):
    width = out_weight.shape[1]

    def ordered(own, other, axis):
        first = lax.axis_index(axis) == 0
        return jnp.where(first, own, other), jnp.where(first, other, own)

    pair = jnp.concatenate(ordered(out_weight, shift(out_weight, "zl", 1), "zl"), axis=1)
    low, high = ordered(pair, shift(pair, "core", 1), "core")
    return jnp.concatenate(
        [low[:, :width], high[:, :width], low[:, width:], high[:, width:]], axis=1
    )


def shards(
    query_rows,
    key_rows,
    value_rows,
    forget,
    head_state,
    out_weight,
    route_ids,
    route_gate,
    gate_weight,
    up_weight,
    down_weight,
):
    steps, rows, _ = query_rows.shape
    blocks = lax.axis_size("y") * lax.axis_size("zp")
    experts = blocks
    capacity = rows // 2
    head = lax.axis_index("head")

    gate, up, down = (
        (w[0], shift(w[0], "core", 1)) for w in (gate_weight, up_weight, down_weight)
    )
    columns = block_columns(out_weight)
    width = columns.shape[1]
    features = width * blocks

    attended, state_out = attention(query_rows, key_rows, value_rows, forget, head_state)

    depth = attended.shape[1]
    ids = jnp.pad(route_ids.reshape(steps * rows, 2).astype(BF16), ((0, 0), (0, LANES - 2)))
    peers = spread(jnp.concatenate([attended, ids], axis=1), BLOCKS)
    peers = peers.reshape(blocks, steps, rows, depth + LANES)
    peer_ids = peers[..., depth : depth + 2].astype(jnp.int32)
    peers = jnp.transpose(peers[..., :depth], (1, 2, 0, 3)).reshape(steps * rows * blocks, depth)
    partial = jnp.dot(peers, columns, preferred_element_type=F32)
    partial = partial.reshape(steps, rows * blocks, width)

    def of_step(array, axis, there=head):
        return lax.dynamic_index_in_dim(array, there, axis, keepdims=False)

    projected = of_step(partial, 0)
    for distance in range(1, steps):
        there = lax.rem(head + distance, steps)
        projected = projected + shift(of_step(partial, 0, there), "head", distance)
    projected = projected.astype(BF16).reshape(rows, blocks, width)

    placed = jnp.sum(place(of_step(peer_ids, 1), experts, capacity), axis=-1)
    packed = sum(
        placed[:, :, :, r, None] * projected[r].astype(F32)[None, None] for r in range(rows)
    ).astype(BF16)
    packed = lax.all_to_all(packed, BLOCKS, split_axis=0, concat_axis=0, tiled=True)
    piece = jnp.transpose(packed, (1, 2, 0, 3)).reshape(capacity * blocks, features)

    result = scatter_block(expert_ffn(gather_block(piece), gate, up, down))

    result = jnp.transpose(result.reshape(capacity, blocks, features), (1, 0, 2))
    mixed = jnp.transpose(projected, (1, 0, 2)).reshape(blocks, capacity, 2 * width)
    result = lax.all_to_all(
        jnp.concatenate([result, mixed], axis=2), BLOCKS, split_axis=0, concat_axis=0, tiled=True
    )
    mixed = result[..., features:].reshape(blocks, rows, width)
    mixed = jnp.transpose(mixed, (1, 0, 2)).reshape(rows, features)
    weights = jnp.sum(
        place(of_step(route_ids, 0), experts, capacity) * of_step(route_gate, 0), axis=-1
    )
    combined = jnp.einsum(
        "esr,esd->rd", weights, result[..., :features].astype(F32), precision=EXACT
    ).astype(BF16)
    both = spread(jnp.concatenate([mixed, combined], axis=0), "head")
    return both[:, :rows], both[:, rows:], state_out


def solution(mesh):
    shape = dict(mesh.shape)
    heads, peers = shape["head"], shape["expert"]
    split = (4, peers // 16, 2, 2)
    fine = Mesh(mesh.devices.reshape((heads,) + split), ("head",) + EXPERT)
    return jax.shard_map(
        shards,
        mesh=fine,
        in_specs=(
            P(None, EXPERT, "head"),
            P(None, EXPERT, "head"),
            P(None, EXPERT, "head"),
            P("head"),
            P(EXPERT, "head", None, None),
            P("head", EXPERT),
            P(None, EXPERT, None),
            P(None, EXPERT, None),
            P(EXPERT, None, "head"),
            P(EXPERT, None, "head"),
            P(EXPERT, "head", None),
        ),
        out_specs=(
            P(None, EXPERT, None),
            P(None, EXPERT, None),
            P(EXPERT, "head", None, None),
        ),
        check_vma=False,
    )
```

```python
import functools

import jax
import jax.numpy as jnp
from jax import lax
from jax.experimental import pallas as pl
from jax.experimental.pallas import tpu as pltpu
from jax.sharding import Mesh, PartitionSpec as P

BLOCKS = ("y", "zp")
EXPERT = ("y", "zp", "zl", "core")
BF16 = jnp.bfloat16
F32 = jnp.float32
LANES = 128
EXACT = lax.Precision.HIGHEST


def shift(array, axis, distance):
    size = lax.axis_size(axis)
    pairs = [(i, (i + distance) % size) for i in range(size)]
    return lax.ppermute(array, axis, pairs)


def spread(array, axis):
    size = lax.axis_size(axis)
    copies = jnp.broadcast_to(array[None], (size,) + array.shape)
    return lax.all_to_all(copies, axis, split_axis=0, concat_axis=0, tiled=True)


def split(array):
    high = array.astype(BF16)
    return high, (array - high.astype(F32)).astype(BF16)


def attend_kernel(steps, rows, forget_ref, query_ref, key_ref, value_ref, state_ref, out_ref):
    rate = forget_ref[pl.program_id(0)]
    query, key, value = query_ref[...], key_ref[...], value_ref[...]
    count = steps * rows
    row_of = lax.broadcasted_iota(jnp.int32, (count, 1), 0)
    step_of = (row_of // rows).astype(F32)
    member = row_of % rows
    from_state = jnp.zeros(out_ref.shape, F32)
    for r in range(rows):
        product = jnp.dot(query, state_ref[r, 0], preferred_element_type=F32)
        from_state += jnp.where(member == r, product, 0.0)
    one = lax.broadcasted_iota(jnp.int32, (count, count), 0)
    other = lax.broadcasted_iota(jnp.int32, (count, count), 1)
    lag = one // rows - other // rows
    seen = (lag >= 0) & (one % rows == other % rows)
    scale = jnp.where(seen, jnp.exp(-rate * jnp.maximum(lag, 0).astype(F32)), 0.0)
    scores = across_lanes(query, key) * scale
    from_steps = sum(jnp.dot(s, value, preferred_element_type=F32) for s in split(scores))
    out_ref[...] = (jnp.exp(-rate * (step_of + 1.0)) * from_state + from_steps).astype(BF16)


def attend(query_rows, key_rows, value_rows, forget, head_state):
    steps, rows, width = query_rows.shape
    heads = forget.shape[0]
    size = width // heads
    count = steps * rows
    lane_block = pl.BlockSpec((count, size), lambda i: (0, i))
    return pl.pallas_call(
        functools.partial(attend_kernel, steps, rows),
        grid=(heads,),
        in_specs=[
            pl.BlockSpec(memory_space=pltpu.SMEM),
            lane_block,
            lane_block,
            lane_block,
            pl.BlockSpec((rows, 1, size, size), lambda i: (0, i, 0, 0)),
        ],
        out_specs=lane_block,
        out_shape=jax.ShapeDtypeStruct((count, width), BF16),
    )(forget, *(a.reshape(count, width) for a in (query_rows, key_rows, value_rows)), head_state)


def last_state(key_rows, value_rows, forget, head_state):
    steps, rows, width = key_rows.shape
    heads = forget.shape[0]
    shape = (steps, rows, heads, width // heads)
    power = jnp.exp(-forget[None, :] * jnp.arange(steps + 1, dtype=F32)[:, None])
    scaled = key_rows.reshape(shape).astype(F32) * power[steps - 1 :: -1][:steps, None, :, None]
    state = power[steps][None, :, None, None] * head_state.astype(F32) + jnp.einsum(
        "trhi,trhj->rhij", scaled, value_rows.reshape(shape).astype(F32), precision=EXACT
    )
    return state.astype(BF16)


def place(ids, experts, capacity):
    rows = ids.shape[-2]
    flat = ids.reshape(ids.shape[:-2] + (rows * 2,))
    onehot = (flat[..., None] == jnp.arange(experts, dtype=jnp.int32)).astype(jnp.int32)
    ranked = jnp.cumsum(onehot, axis=-2) - 1
    landed = onehot[..., None] * (
        ranked[..., None] == jnp.arange(capacity, dtype=jnp.int32)
    ).astype(jnp.int32)
    landed = jnp.moveaxis(landed, (-2, -1), (0, 1)).astype(F32)
    return landed.reshape(landed.shape[:-1] + (rows, 2))


def gather_block(own):
    half = own.shape[0] // 2
    left, right, across = shift(own, "head", 1), shift(own, "head", -1), shift(own, "zl", 1)

    def halves(one, other):
        return jnp.concatenate([one, other], axis=0)

    by_left = shift(halves(left[:half], across[:half]), "head", 1)
    by_right = shift(halves(right[half:], across[half:]), "head", -1)
    by_across = shift(halves(left[half:], right[:half]), "zl", 1)
    last_left = shift(by_left[half:], "head", 1)
    last_right = shift(by_right[half:], "head", -1)
    return [own, left, right, across, by_left, by_right, by_across, last_left, last_right]


def scatter_block(parts):
    own, left, right, across, by_left, by_right, by_across, last_left, last_right = parts
    half = own.shape[0] // 2

    def add(*terms):
        return sum(t.astype(F32) for t in terms).astype(BF16)

    def halves(one, other):
        return jnp.concatenate([one, other], axis=0)

    from_right = shift(last_left, "head", -1)
    from_left = shift(last_right, "head", 1)
    by_left = halves(by_left[:half], add(by_left[half:], from_right))
    by_right = halves(by_right[:half], add(by_right[half:], from_left))
    from_right = shift(by_left, "head", -1)
    from_left = shift(by_right, "head", 1)
    from_across = shift(by_across, "zl", 1)
    left = add(left, halves(from_right[:half], from_across[:half]))
    right = add(right, halves(from_across[half:], from_left[:half]))
    across = add(across, halves(from_right[half:], from_left[half:]))
    return add(own, shift(left, "head", -1), shift(right, "head", 1), shift(across, "zl", 1))


def across_lanes(one, other):
    return lax.dot_general(one, other, (((1,), (1,)), ((), ())), preferred_element_type=F32)


def ffn_kernel(count, inner, *refs):
    rows, refs = refs[:count], refs[count:]
    wide, down, refs = refs[:4], refs[4:6], refs[6:]
    outs, (sums, hidden) = refs[:count], refs[count:]
    step = pl.program_id(0)

    @pl.when(step < inner)
    def _():
        block = jnp.concatenate([r[...] for r in rows], axis=0)
        weights = jnp.concatenate([w[...] for w in wide], axis=0)
        product = across_lanes(block, weights)

        @pl.when(step == 0)
        def _():
            sums[...] = product

        @pl.when(step > 0)
        def _():
            sums[...] += product

    @pl.when(step == inner - 1)
    def _():
        value = sums[...]
        width = value.shape[1] // 2
        gated, lifted = value[:, :width], value[:, width:]
        hidden[...] = (gated / (1.0 + jnp.exp(-gated)) * lifted).astype(BF16)

    @pl.when(step >= inner)
    def _():
        weights = jnp.concatenate([w[...] for w in down], axis=0)
        total = jnp.dot(hidden[...], weights, preferred_element_type=F32).astype(BF16)
        start = 0
        for out in outs:
            out[...] = total[start : start + out.shape[0]]
            start += out.shape[0]


def expert_ffn(parts, gate, up, down):
    width, features = gate[0].shape
    total_rows = sum(p.shape[0] for p in parts)
    tile = min(features, 1024)
    inner = features // tile

    def first(i):
        return (0, jnp.minimum(i, inner - 1))

    def second(i):
        return (0, jnp.maximum(i - inner, 0))

    return pl.pallas_call(
        functools.partial(ffn_kernel, len(parts), inner),
        grid=(2 * inner,),
        in_specs=[pl.BlockSpec((p.shape[0], tile), first) for p in parts]
        + [pl.BlockSpec((width, tile), first)] * 4
        + [pl.BlockSpec((width, tile), second)] * 2,
        out_specs=[pl.BlockSpec((p.shape[0], tile), second) for p in parts],
        out_shape=[jax.ShapeDtypeStruct(p.shape, BF16) for p in parts],
        scratch_shapes=[
            pltpu.VMEM((total_rows, 4 * width), F32),
            pltpu.VMEM((total_rows, 2 * width), BF16),
        ],
        compiler_params=pltpu.CompilerParams(vmem_limit_bytes=32 * 1024 * 1024),
        cost_estimate=pl.CostEstimate(
            flops=12 * total_rows * features * width,
            bytes_accessed=12 * features * width + 4 * total_rows * features,
            transcendentals=2 * total_rows * width,
        ),
    )(*parts, *gate, *up, *down)


def block_columns(out_weight):
    width = out_weight.shape[1]

    def ordered(own, other, axis):
        first = lax.axis_index(axis) == 0
        return jnp.where(first, own, other), jnp.where(first, other, own)

    pair = jnp.concatenate(ordered(out_weight, shift(out_weight, "zl", 1), "zl"), axis=1)
    low, high = ordered(pair, shift(pair, "core", 1), "core")
    return jnp.concatenate(
        [low[:, :width], high[:, :width], low[:, width:], high[:, width:]], axis=1
    )


def shards(
    query_rows,
    key_rows,
    value_rows,
    forget,
    head_state,
    out_weight,
    route_ids,
    route_gate,
    gate_weight,
    up_weight,
    down_weight,
):
    steps, rows, _ = query_rows.shape
    blocks = lax.axis_size("y") * lax.axis_size("zp")
    experts = blocks
    capacity = rows // 2
    head = lax.axis_index("head")

    gate, up, down = (
        (w, shift(w, "core", 1)) for w in (gate_weight[0].T, up_weight[0].T, down_weight[0])
    )
    columns = block_columns(out_weight)
    width = columns.shape[1]
    features = width * blocks

    attended = attend(query_rows, key_rows, value_rows, forget, head_state)
    state_out = last_state(key_rows, value_rows, forget, head_state)

    depth = attended.shape[1]
    ids = jnp.pad(route_ids.reshape(steps * rows, 2).astype(BF16), ((0, 0), (0, LANES - 2)))
    peers = spread(jnp.concatenate([attended, ids], axis=1), BLOCKS)
    peers, gate, up, down = lax.optimization_barrier((peers, gate, up, down))
    peers = peers.reshape(blocks, steps, rows, depth + LANES)
    peer_ids = peers[..., depth : depth + 2].astype(jnp.int32)
    peers = jnp.transpose(peers[..., :depth], (1, 2, 0, 3)).reshape(steps * rows * blocks, depth)
    partial = jnp.dot(peers, columns, preferred_element_type=F32)
    partial = partial.reshape(steps, rows * blocks, width)

    def of_step(array, axis, there=head):
        return lax.dynamic_index_in_dim(array, there, axis, keepdims=False)

    projected = of_step(partial, 0)
    for distance in range(1, steps):
        there = lax.rem(head + distance, steps)
        projected = projected + shift(of_step(partial, 0, there), "head", distance)
    projected = projected.astype(BF16).reshape(rows, blocks, width)

    placed = jnp.sum(place(of_step(peer_ids, 1), experts, capacity), axis=-1)
    packed = sum(
        placed[:, :, :, r, None] * projected[r].astype(F32)[None, None] for r in range(rows)
    ).astype(BF16)
    packed = lax.all_to_all(packed, BLOCKS, split_axis=0, concat_axis=0, tiled=True)
    piece = jnp.transpose(packed, (1, 2, 0, 3)).reshape(capacity * blocks, features)

    result = scatter_block(expert_ffn(gather_block(piece), gate, up, down))

    result = jnp.transpose(result.reshape(capacity, blocks, features), (1, 0, 2))
    mixed = jnp.transpose(projected, (1, 0, 2)).reshape(blocks, capacity, 2 * width)
    result = lax.all_to_all(
        jnp.concatenate([result, mixed], axis=2), BLOCKS, split_axis=0, concat_axis=0, tiled=True
    )
    mixed = result[..., features:].reshape(blocks, rows, width)
    mixed = jnp.transpose(mixed, (1, 0, 2)).reshape(rows, features)
    weights = jnp.sum(
        place(of_step(route_ids, 0), experts, capacity) * of_step(route_gate, 0), axis=-1
    )
    combined = jnp.einsum(
        "esr,esd->rd", weights, result[..., :features].astype(F32), precision=EXACT
    ).astype(BF16)
    both = spread(jnp.concatenate([mixed, combined], axis=0), "head")
    return both[:, :rows], both[:, rows:], state_out


def solution(mesh):
    shape = dict(mesh.shape)
    heads, peers = shape["head"], shape["expert"]
    split = (4, peers // 16, 2, 2)
    fine = Mesh(mesh.devices.reshape((heads,) + split), ("head",) + EXPERT)
    return jax.shard_map(
        shards,
        mesh=fine,
        in_specs=(
            P(None, EXPERT, "head"),
            P(None, EXPERT, "head"),
            P(None, EXPERT, "head"),
            P("head"),
            P(EXPERT, "head", None, None),
            P("head", EXPERT),
            P(None, EXPERT, None),
            P(None, EXPERT, None),
            P(EXPERT, None, "head"),
            P(EXPERT, None, "head"),
            P(EXPERT, "head", None),
        ),
        out_specs=(
            P(None, EXPERT, None),
            P(None, EXPERT, None),
            P(EXPERT, "head", None, None),
        ),
        check_vma=False,
    )
```

```python
import functools

import jax
import jax.numpy as jnp
from jax import lax
from jax.experimental import pallas as pl
from jax.experimental.pallas import tpu as pltpu
from jax.sharding import Mesh, PartitionSpec as P

BLOCKS = ("yh", "yl", "zp")
PEERS = ("yh", "zp")
EXPERT = BLOCKS + ("zl", "core")
BF16 = jnp.bfloat16
F32 = jnp.float32
LANES = 128
EXACT = lax.Precision.HIGHEST


def shift(array, axis, distance):
    size = lax.axis_size(axis)
    pairs = [(i, (i + distance) % size) for i in range(size)]
    return lax.ppermute(array, axis, pairs)


def spread(array, axis):
    size = lax.axis_size(axis)
    copies = jnp.broadcast_to(array[None], (size,) + array.shape)
    return lax.all_to_all(copies, axis, split_axis=0, concat_axis=0, tiled=True)


def attention(query_rows, key_rows, value_rows, forget, head_state):
    steps, rows, width = query_rows.shape
    heads = forget.shape[0]
    size = width // heads
    shape = (steps, rows, heads, size)
    query, key, value = (a.reshape(shape) for a in (query_rows, key_rows, value_rows))
    times = jnp.arange(steps, dtype=F32)
    power = jnp.exp(-forget[None, :] * jnp.arange(steps + 1, dtype=F32)[:, None])
    lag = times[:, None] - times[None, :]
    causal = jnp.where(
        lag[..., None] >= 0, jnp.exp(-forget * jnp.maximum(lag, 0.0)[..., None]), 0.0
    )
    from_state = jnp.einsum("trhi,rhij->trhj", query, head_state, preferred_element_type=F32)
    scores = jnp.einsum("trhi,srhi->tsrh", query, key, preferred_element_type=F32)
    scores = scores * causal[:, :, None, :]
    value_float = value.astype(F32)
    from_steps = sum(scores[:, s, :, :, None] * value_float[s][None] for s in range(steps))
    attended = power[1:, None, :, None] * from_state + from_steps
    attended = attended.astype(BF16).reshape(steps * rows, width)
    scaled_key = key.astype(F32) * power[steps - 1 :: -1][:steps, None, :, None]
    state = power[steps][None, :, None, None] * head_state.astype(F32) + jnp.einsum(
        "trhi,trhj->rhij", scaled_key, value_float, precision=EXACT
    )
    return attended, state.astype(BF16)


def place(ids, experts, capacity):
    rows = ids.shape[-2]
    flat = ids.reshape(ids.shape[:-2] + (rows * 2,))
    onehot = (flat[..., None] == jnp.arange(experts, dtype=jnp.int32)).astype(jnp.int32)
    ranked = jnp.cumsum(onehot, axis=-2) - 1
    landed = onehot[..., None] * (
        ranked[..., None] == jnp.arange(capacity, dtype=jnp.int32)
    ).astype(jnp.int32)
    landed = jnp.moveaxis(landed, (-2, -1), (0, 1)).astype(F32)
    return landed.reshape(landed.shape[:-1] + (rows, 2))


def gather_block(own):
    half = own.shape[0] // 2
    left, right, across = shift(own, "head", 1), shift(own, "head", -1), shift(own, "zl", 1)

    def halves(one, other):
        return jnp.concatenate([one, other], axis=0)

    by_left = shift(halves(left[:half], across[:half]), "head", 1)
    by_right = shift(halves(right[half:], across[half:]), "head", -1)
    by_across = shift(halves(left[half:], right[:half]), "zl", 1)
    last_left = shift(by_left[half:], "head", 1)
    last_right = shift(by_right[half:], "head", -1)
    return [own, left, right, across, by_left, by_right, by_across, last_left, last_right]


def scatter_block(parts):
    own, left, right, across, by_left, by_right, by_across, last_left, last_right = parts
    half = own.shape[0] // 2

    def add(*terms):
        return sum(t.astype(F32) for t in terms).astype(BF16)

    def halves(one, other):
        return jnp.concatenate([one, other], axis=0)

    from_right = shift(last_left, "head", -1)
    from_left = shift(last_right, "head", 1)
    by_left = halves(by_left[:half], add(by_left[half:], from_right))
    by_right = halves(by_right[:half], add(by_right[half:], from_left))
    from_right = shift(by_left, "head", -1)
    from_left = shift(by_right, "head", 1)
    from_across = shift(by_across, "zl", 1)
    left = add(left, halves(from_right[:half], from_across[:half]))
    right = add(right, halves(from_across[half:], from_left[:half]))
    across = add(across, halves(from_right[half:], from_left[half:]))
    return add(own, shift(left, "head", -1), shift(right, "head", 1), shift(across, "zl", 1))


def across_lanes(one, other):
    return lax.dot_general(one, other, (((1,), (1,)), ((), ())), preferred_element_type=F32)


def ffn_kernel(count, inner, *refs):
    rows, refs = refs[:count], refs[count:]
    wide, down, refs = refs[:4], refs[4:6], refs[6:]
    outs, (sums, hidden) = refs[:count], refs[count:]
    step = pl.program_id(0)

    @pl.when(step < inner)
    def _():
        block = jnp.concatenate([r[...] for r in rows], axis=0)
        weights = jnp.concatenate([w[...] for w in wide], axis=0)
        product = across_lanes(block, weights)

        @pl.when(step == 0)
        def _():
            sums[...] = product

        @pl.when(step > 0)
        def _():
            sums[...] += product

    @pl.when(step == inner - 1)
    def _():
        value = sums[...]
        width = value.shape[1] // 2
        gated, lifted = value[:, :width], value[:, width:]
        hidden[...] = (gated / (1.0 + jnp.exp(-gated)) * lifted).astype(BF16)

    @pl.when(step >= inner)
    def _():
        weights = jnp.concatenate([w[...] for w in down], axis=0)
        total = jnp.dot(hidden[...], weights, preferred_element_type=F32).astype(BF16)
        start = 0
        for out in outs:
            out[...] = total[start : start + out.shape[0]]
            start += out.shape[0]


def expert_ffn(parts, gate, up, down):
    width, features = gate[0].shape
    total_rows = sum(p.shape[0] for p in parts)
    tile = min(features, 2048)
    inner = features // tile

    def first(i):
        return (0, jnp.minimum(i, inner - 1))

    def second(i):
        return (0, jnp.maximum(i - inner, 0))

    return pl.pallas_call(
        functools.partial(ffn_kernel, len(parts), inner),
        grid=(2 * inner,),
        in_specs=[pl.BlockSpec((p.shape[0], tile), first) for p in parts]
        + [pl.BlockSpec((width, tile), first)] * 4
        + [pl.BlockSpec((width, tile), second)] * 2,
        out_specs=[pl.BlockSpec((p.shape[0], tile), second) for p in parts],
        out_shape=[jax.ShapeDtypeStruct(p.shape, BF16) for p in parts],
        scratch_shapes=[
            pltpu.VMEM((total_rows, 4 * width), F32),
            pltpu.VMEM((total_rows, 2 * width), BF16),
        ],
        compiler_params=pltpu.CompilerParams(vmem_limit_bytes=28 * 1024 * 1024),
        cost_estimate=pl.CostEstimate(
            flops=12 * total_rows * features * width,
            bytes_accessed=12 * features * width + 4 * total_rows * features,
            transcendentals=2 * total_rows * width,
        ),
    )(*parts, *gate, *up, *down)


def peer_columns(columns):
    def ordered(shape, own, other, axis, where):
        index = lax.axis_index(axis)
        whole = jnp.zeros(shape, own.dtype)
        for part, position in ((own, index), (other, 1 - index)):
            whole = lax.dynamic_update_slice_in_dim(whole, part, position, where)
        return whole

    here, depth = columns.shape
    columns = columns[None]
    columns = ordered((2, here, depth), columns, shift(columns, "zl", 1), "zl", 0)[None]
    columns = ordered((2, 2, here, depth), columns, shift(columns, "yl", 1), "yl", 0)[:, :, None]
    columns = ordered((2, 2, 2, here, depth), columns, shift(columns, "core", 1), "core", 2)
    return columns.reshape(8 * here, depth)


def shards(
    query_rows,
    key_rows,
    value_rows,
    forget,
    head_state,
    out_weight,
    route_ids,
    route_gate,
    gate_weight,
    up_weight,
    down_weight,
):
    steps, rows, depth = query_rows.shape
    peers = lax.axis_size("yh") * lax.axis_size("zp")
    blocks = 2 * peers
    experts = blocks
    capacity = rows // 2
    head = lax.axis_index("head")

    gate, up, down = (
        (w, shift(w, "core", 1)) for w in (gate_weight[0].T, up_weight[0].T, down_weight[0])
    )
    columns = peer_columns(out_weight.T)
    width = columns.shape[0]
    piece_width = width // 2
    features = width * peers

    attended, state_out = attention(query_rows, key_rows, value_rows, forget, head_state)

    ids = jnp.pad(route_ids.reshape(steps * rows, 2).astype(BF16), ((0, 0), (0, LANES - 2)))
    gathered = spread(jnp.concatenate([attended, ids], axis=1), PEERS)
    gathered, gate, up, down = lax.optimization_barrier((gathered, gate, up, down))
    gathered = gathered.reshape(peers * steps * rows, depth + LANES)
    partial = lax.dot_general(
        gathered[:, :depth], columns, (((1,), (1,)), ((), ())), preferred_element_type=F32
    )
    partial = partial.reshape(peers, steps, rows, width)
    peer_ids = gathered[:, depth : depth + 2].astype(jnp.int32).reshape(peers, steps, rows, 2)

    def of_step(array, axis, there=head):
        return lax.dynamic_index_in_dim(array, there, axis, keepdims=False)

    projected = of_step(partial, 1)
    for distance in range(1, steps):
        there = lax.rem(head + distance, steps)
        projected = projected + shift(of_step(partial, 1, there), "head", distance)
    projected = projected.astype(BF16)

    placed = jnp.sum(place(of_step(peer_ids, 1), experts, capacity), axis=-1)
    packed = sum(
        placed[:, :, :, r, None] * projected[:, r].astype(F32)[None, None] for r in range(rows)
    ).astype(BF16)
    packed = lax.all_to_all(packed, BLOCKS, split_axis=0, concat_axis=0, tiled=True)
    packed = packed.reshape(2, 2, peers // 2, capacity, peers, 2, piece_width)
    piece = jnp.transpose(packed, (1, 3, 4, 0, 5, 2, 6)).reshape(capacity * blocks, features)

    pieces = gather_block(piece)
    pieces[-1], state_out = lax.optimization_barrier((pieces[-1], state_out))
    result = scatter_block(expert_ffn(pieces, gate, up, down))

    result = result.reshape(2, capacity, 2, peers // 2, features)
    result = jnp.transpose(result, (2, 0, 3, 1, 4)).reshape(blocks, capacity, features)
    mixed = projected.reshape(2, 1, peers // 2, capacity, 2 * width)
    mixed = jnp.broadcast_to(mixed, (2, 2) + mixed.shape[2:]).reshape(blocks, capacity, 2 * width)
    result = lax.all_to_all(
        jnp.concatenate([result, mixed], axis=2), BLOCKS, split_axis=0, concat_axis=0, tiled=True
    )
    mixed = result[..., features:].reshape(2, 2, peers // 2, rows, 2, piece_width)
    mixed = lax.dynamic_index_in_dim(mixed, lax.axis_index("yl"), 1, keepdims=False)
    mixed = jnp.transpose(mixed, (2, 0, 3, 1, 4)).reshape(rows, features)
    weights = jnp.sum(
        place(of_step(route_ids, 0), experts, capacity) * of_step(route_gate, 0), axis=-1
    )
    combined = jnp.einsum(
        "esr,esd->rd", weights, result[..., :features].astype(F32), precision=EXACT
    ).astype(BF16)
    both = spread(jnp.concatenate([mixed, combined], axis=0), "head")
    return both[:, :rows], both[:, rows:], state_out


def solution(mesh):
    shape = dict(mesh.shape)
    heads, peers = shape["head"], shape["expert"]
    split = (2, 2, peers // 16, 2, 2)
    fine = Mesh(mesh.devices.reshape((heads,) + split), ("head",) + EXPERT)
    return jax.shard_map(
        shards,
        mesh=fine,
        in_specs=(
            P(None, EXPERT, "head"),
            P(None, EXPERT, "head"),
            P(None, EXPERT, "head"),
            P("head"),
            P(EXPERT, "head", None, None),
            P("head", EXPERT),
            P(None, EXPERT, None),
            P(None, EXPERT, None),
            P(EXPERT, None, "head"),
            P(EXPERT, None, "head"),
            P(EXPERT, "head", None),
        ),
        out_specs=(
            P(None, EXPERT, None),
            P(None, EXPERT, None),
            P(EXPERT, "head", None, None),
        ),
        check_vma=False,
    )
```

```python
import functools

import jax
import jax.numpy as jnp
from jax import lax
from jax.experimental import pallas as pl
from jax.experimental.pallas import tpu as pltpu
from jax.sharding import Mesh, PartitionSpec as P

BLOCKS = ("yh", "yl", "zp")
PEERS = ("yh", "zp")
EXPERT = BLOCKS + ("zl", "core")
BF16 = jnp.bfloat16
F32 = jnp.float32
LANES = 128
EXACT = lax.Precision.HIGHEST


def shift(array, axis, distance):
    size = lax.axis_size(axis)
    pairs = [(i, (i + distance) % size) for i in range(size)]
    return lax.ppermute(array, axis, pairs)


def spread(array, axis):
    size = lax.axis_size(axis)
    copies = jnp.broadcast_to(array[None], (size,) + array.shape)
    return lax.all_to_all(copies, axis, split_axis=0, concat_axis=0, tiled=True)


def split(array):
    high = array.astype(BF16)
    return high, (array - high.astype(F32)).astype(BF16)


def attend_kernel(capacity, forget_ref, ids_ref, *refs):
    sources, out_ref, flat, landed, arrived = refs[:4], refs[4], refs[5], refs[6:10], refs[10]
    copies = [
        pltpu.make_async_copy(source, target, arrived.at[i])
        for i, (source, target) in enumerate(zip(sources, landed))
    ]
    for copy in copies:
        copy.start()
    query_ref, key_ref, value_ref, state_ref = landed
    steps, rows, width = query_ref.shape
    heads, size = state_ref.shape[1], state_ref.shape[2]
    count = steps * rows
    shape = (count, LANES)
    row, lane = (lax.broadcasted_iota(jnp.int32, shape, i) for i in range(2))
    tail = jnp.zeros(shape, jnp.int32)
    for t in range(steps):
        ids = [ids_ref[t, i // 2, i % 2] for i in range(2 * rows)]
        for i in range(2 * rows):
            slot = sum((jnp.where(ids[j] == ids[i], 1, 0) for j in range(i)), jnp.int32(0))
            here = (row == t * rows + i // 2) & (lane == i % 2)
            tail = jnp.where(here, ids[i] * capacity + slot, tail)
    tail = tail.astype(F32).astype(BF16)
    for copy in copies:
        copy.wait()
    for i, ref in enumerate((query_ref, key_ref, value_ref)):
        for t in range(steps):
            flat[i, t * rows : (t + 1) * rows] = ref[t].astype(F32)
    row_of = lax.broadcasted_iota(jnp.int32, (count, 1), 0)
    age = (row_of // rows + 1).astype(F32)
    member = row_of % rows
    one = lax.broadcasted_iota(jnp.int32, (count, count), 0)
    other = lax.broadcasted_iota(jnp.int32, (count, count), 1)
    lag = one // rows - other // rows
    seen = (lag >= 0) & (one % rows == other % rows)
    gap = jnp.maximum(lag, 0).astype(F32)
    for h in range(heads):
        lanes = slice(h * size, (h + 1) * size)
        rate = forget_ref[h]
        query, key, value = (flat[i, :, lanes].astype(BF16) for i in range(3))
        from_state = jnp.zeros((count, size), F32)
        for r in range(rows):
            product = jnp.dot(query, state_ref[r, h], preferred_element_type=F32)
            from_state += jnp.where(member == r, product, 0.0)
        scores = across_lanes(query, key) * jnp.where(seen, jnp.exp(-rate * gap), 0.0)
        from_steps = sum(jnp.dot(s, value, preferred_element_type=F32) for s in split(scores))
        attended = (jnp.exp(-rate * age) * from_state + from_steps).astype(BF16)
        for i in range(out_ref.shape[0]):
            out_ref[i, :, lanes] = attended
    for i in range(out_ref.shape[0]):
        out_ref[i, :, width:] = tail


def attend(query_rows, key_rows, value_rows, forget, head_state, route_ids, capacity, copies):
    steps, rows, width = query_rows.shape
    count = steps * rows
    whole = pl.BlockSpec(memory_space=pltpu.VMEM)
    return pl.pallas_call(
        functools.partial(attend_kernel, capacity),
        in_specs=[pl.BlockSpec(memory_space=pltpu.SMEM)] * 2
        + [pl.BlockSpec(memory_space=pltpu.HBM)] * 4,
        out_specs=whole,
        out_shape=jax.ShapeDtypeStruct((copies, count, width + LANES), BF16),
        scratch_shapes=[pltpu.VMEM((3, count, width), F32)]
        + [pltpu.VMEM(query_rows.shape, BF16)] * 3
        + [pltpu.VMEM(head_state.shape, BF16), pltpu.SemaphoreType.DMA((4,))],
        compiler_params=pltpu.CompilerParams(vmem_limit_bytes=54 * 1024 * 1024),
    )(forget, route_ids, query_rows, key_rows, value_rows, head_state)


def state_kernel(forget_ref, key_ref, value_ref, state_ref, out_ref, flat):
    steps, rows, width = key_ref.shape
    heads, size = state_ref.shape[1], state_ref.shape[2]
    count = steps * rows
    for i, ref in enumerate((key_ref, value_ref)):
        for t in range(steps):
            flat[i, t * rows : (t + 1) * rows] = ref[t].astype(F32)
    row_of = lax.broadcasted_iota(jnp.int32, (count, 1), 0)
    left = (steps - 1 - row_of // rows).astype(F32)
    member = row_of % rows
    for h in range(heads):
        lanes = slice(h * size, (h + 1) * size)
        rate = forget_ref[h]
        decay = jnp.exp(-rate * jnp.full((1, 1), steps, F32))
        scaled = flat[0, :, lanes] * jnp.exp(-rate * left)
        value = flat[1, :, lanes].astype(BF16)
        values = jnp.concatenate([value, value], axis=0)
        for r in range(rows):
            terms = jnp.concatenate(split(jnp.where(member == r, scaled, 0.0)), axis=0)
            added = lax.dot_general(
                terms, values, (((0,), (0,)), ((), ())), preferred_element_type=F32
            )
            out_ref[r, h] = (decay * state_ref[r, h].astype(F32) + added).astype(BF16)


def last_state(key_rows, value_rows, forget, head_state):
    steps, rows, width = key_rows.shape
    whole = pl.BlockSpec(memory_space=pltpu.VMEM)
    return pl.pallas_call(
        state_kernel,
        in_specs=[pl.BlockSpec(memory_space=pltpu.SMEM)] + [whole] * 3,
        out_specs=whole,
        out_shape=jax.ShapeDtypeStruct(head_state.shape, BF16),
        scratch_shapes=[pltpu.VMEM((2, steps * rows, width), F32)],
        compiler_params=pltpu.CompilerParams(vmem_limit_bytes=12 * 1024 * 1024),
        cost_estimate=pl.CostEstimate(
            flops=4 * steps * rows * head_state.size,
            bytes_accessed=4 * head_state.size,
            transcendentals=0,
        ),
    )(forget, key_rows, value_rows, head_state)


def place(ids, experts, capacity):
    rows = ids.shape[-2]
    flat = ids.reshape(ids.shape[:-2] + (rows * 2,))
    onehot = (flat[..., None] == jnp.arange(experts, dtype=jnp.int32)).astype(jnp.int32)
    ranked = jnp.cumsum(onehot, axis=-2) - 1
    landed = onehot[..., None] * (
        ranked[..., None] == jnp.arange(capacity, dtype=jnp.int32)
    ).astype(jnp.int32)
    landed = jnp.moveaxis(landed, (-2, -1), (0, 1)).astype(F32)
    return landed.reshape(landed.shape[:-1] + (rows, 2))


def gather_block(own):
    half = own.shape[0] // 2
    left, right, across = shift(own, "head", 1), shift(own, "head", -1), shift(own, "zl", 1)

    def halves(one, other):
        return jnp.concatenate([one, other], axis=0)

    by_left = shift(halves(left[:half], across[:half]), "head", 1)
    by_right = shift(halves(right[half:], across[half:]), "head", -1)
    by_across = shift(halves(left[half:], right[:half]), "zl", 1)
    last_left = shift(by_left[half:], "head", 1)
    last_right = shift(by_right[half:], "head", -1)
    return [own, left, right, across, by_left, by_right, by_across, last_left, last_right]


def scatter_block(parts):
    own, left, right, across, by_left, by_right, by_across, last_left, last_right = parts
    half = own.shape[0] // 2

    def add(*terms):
        return sum(t.astype(F32) for t in terms).astype(BF16)

    def halves(one, other):
        return jnp.concatenate([one, other], axis=0)

    from_right = shift(last_left, "head", -1)
    from_left = shift(last_right, "head", 1)
    by_left = halves(by_left[:half], add(by_left[half:], from_right))
    by_right = halves(by_right[:half], add(by_right[half:], from_left))
    from_right = shift(by_left, "head", -1)
    from_left = shift(by_right, "head", 1)
    from_across = shift(by_across, "zl", 1)
    left = add(left, halves(from_right[:half], from_across[:half]))
    right = add(right, halves(from_across[half:], from_left[:half]))
    across = add(across, halves(from_right[half:], from_left[half:]))
    return add(own, shift(left, "head", -1), shift(right, "head", 1), shift(across, "zl", 1))


def across_lanes(one, other):
    return lax.dot_general(one, other, (((1,), (1,)), ((), ())), preferred_element_type=F32)


def ffn_kernel(count, inner, *refs):
    rows, refs = refs[:count], refs[count:]
    wide, down, refs = refs[:4], refs[4:6], refs[6:]
    outs, (sums, hidden) = refs[:count], refs[count:]
    step = pl.program_id(0)

    @pl.when(step < inner)
    def _():
        block = jnp.concatenate([r[...] for r in rows], axis=0)
        weights = jnp.concatenate([w[...] for w in wide], axis=0)
        product = across_lanes(block, weights)

        @pl.when(step == 0)
        def _():
            sums[...] = product

        @pl.when(step > 0)
        def _():
            sums[...] += product

    @pl.when(step == inner - 1)
    def _():
        value = sums[...]
        width = value.shape[1] // 2
        gated, lifted = value[:, :width], value[:, width:]
        hidden[...] = (gated / (1.0 + jnp.exp(-gated)) * lifted).astype(BF16)

    @pl.when(step >= inner)
    def _():
        weights = jnp.concatenate([w[...] for w in down], axis=0)
        total = jnp.dot(hidden[...], weights, preferred_element_type=F32).astype(BF16)
        start = 0
        for out in outs:
            out[...] = total[start : start + out.shape[0]]
            start += out.shape[0]


def expert_ffn(parts, gate, up, down):
    width, features = gate[0].shape
    total_rows = sum(p.shape[0] for p in parts)
    tile = min(features, 3072)
    inner = features // tile

    def first(i):
        return (0, jnp.minimum(i, inner - 1))

    def second(i):
        return (0, jnp.maximum(i - inner, 0))

    return pl.pallas_call(
        functools.partial(ffn_kernel, len(parts), inner),
        grid=(2 * inner,),
        in_specs=[pl.BlockSpec((p.shape[0], tile), first) for p in parts]
        + [pl.BlockSpec((width, tile), first)] * 4
        + [pl.BlockSpec((width, tile), second)] * 2,
        out_specs=[pl.BlockSpec((p.shape[0], tile), second) for p in parts],
        out_shape=[jax.ShapeDtypeStruct(p.shape, BF16) for p in parts],
        scratch_shapes=[
            pltpu.VMEM((total_rows, 4 * width), F32),
            pltpu.VMEM((total_rows, 2 * width), BF16),
        ],
        compiler_params=pltpu.CompilerParams(vmem_limit_bytes=40 * 1024 * 1024),
        cost_estimate=pl.CostEstimate(
            flops=12 * total_rows * features * width,
            bytes_accessed=12 * features * width + 4 * total_rows * features,
            transcendentals=2 * total_rows * width,
        ),
    )(*parts, *gate, *up, *down)


def peer_columns(columns, payload, weights):
    here, depth = columns.shape
    yl, zl, core = (lax.axis_index(axis) == 0 for axis in ("yl", "zl", "core"))
    by_zl, by_yl = shift(columns, "zl", 1), shift(columns, "yl", 1)
    by_both = lax.ppermute(columns, ("yl", "zl"), [(i, 3 - i) for i in range(4)])

    def ordered(first, own, other):
        return jnp.where(first, own, other), jnp.where(first, other, own)

    low, high = ordered(zl, columns, by_zl), ordered(zl, by_yl, by_both)
    first, second = ordered(yl, low[0], high[0]), ordered(yl, low[1], high[1])
    quad = jnp.stack([first[0], second[0], first[1], second[1]])
    quad, weights, _ = lax.optimization_barrier((quad, weights, payload))
    whole = jnp.stack(ordered(core, quad, shift(quad, "core", 1)), axis=1)
    return jnp.pad(whole.reshape(8 * here, depth), ((0, 0), (0, LANES))), weights


def pack_kernel(code_ref, *refs):
    terms, (sum_ref, out_ref, flat) = refs[:-3], refs[-3:]
    peers, rows, width = terms[0].shape
    experts, halves, places, half = out_ref.shape
    for p in range(peers):
        flat[p * rows : (p + 1) * rows] = sum(term[p] for term in terms)
    total = flat[...].astype(BF16)
    sum_ref[...] = total
    shape = (peers * rows, experts * places)
    lane = lax.broadcasted_iota(jnp.int32, shape, 1)
    peer = lax.broadcasted_iota(jnp.int32, shape, 0) // rows
    slot = (lane // peers).astype(F32)
    hit = (slot == code_ref[:, 0:1]) | (slot == code_ref[:, 1:2])
    route = jnp.where(hit & (lane % peers == peer), 1.0, 0.0).astype(BF16)
    packed = lax.dot_general(
        route, total, (((0,), (0,)), ((), ())), preferred_element_type=F32
    ).astype(BF16)
    for e in range(experts):
        for i in range(halves):
            out_ref[e, i] = packed[e * places : (e + 1) * places, i * half : (i + 1) * half]


def pack(codes, terms, experts, capacity):
    peers, rows, width = terms[0].shape
    whole = pl.BlockSpec(memory_space=pltpu.VMEM)
    return pl.pallas_call(
        pack_kernel,
        in_specs=[whole] * (1 + len(terms)),
        out_specs=[whole] * 2,
        out_shape=[
            jax.ShapeDtypeStruct((peers * rows, width), BF16),
            jax.ShapeDtypeStruct((experts, 2, capacity * peers, width // 2), BF16),
        ],
        scratch_shapes=[pltpu.VMEM((peers * rows, width), F32)],
        compiler_params=pltpu.CompilerParams(vmem_limit_bytes=8 * 1024 * 1024),
    )(codes, *terms)


def shards(
    query_rows,
    key_rows,
    value_rows,
    forget,
    head_state,
    out_weight,
    route_ids,
    route_gate,
    gate_weight,
    up_weight,
    down_weight,
):
    steps, rows, depth = query_rows.shape
    peers = lax.axis_size("yh") * lax.axis_size("zp")
    blocks = 2 * peers
    experts = blocks
    capacity = rows // 2
    head = lax.axis_index("head")

    payload = attend(
        query_rows, key_rows, value_rows, forget, head_state, route_ids, capacity, peers
    )
    state_out = last_state(key_rows, value_rows, forget, head_state)
    own = (gate_weight[0].T, up_weight[0].T, down_weight[0])
    columns, own = peer_columns(out_weight.T, payload, own)
    width = columns.shape[0]
    piece_width = width // 2
    features = width * peers
    gathered = lax.all_to_all(payload, PEERS, split_axis=0, concat_axis=0, tiled=True)
    other = tuple(shift(w, "core", 1) for w in own)
    gathered, other = lax.optimization_barrier((gathered, other))
    gate, up, down = zip(own, other)

    partial = lax.dot_general(
        gathered.reshape(peers * steps * rows, depth + LANES),
        columns,
        (((1,), (1,)), ((), ())),
        preferred_element_type=F32,
    ).reshape(peers, steps * rows, width)
    partial = lax.optimization_barrier(partial)

    def of_step(array, axis, there=head, size=1):
        return lax.dynamic_slice_in_dim(array, there * size, size, axis)

    terms = [of_step(partial, 1, size=rows)]
    for distance in range(1, steps):
        there = lax.rem(head + distance, steps)
        terms.append(shift(of_step(partial, 1, there, rows), "head", distance))
    codes = of_step(gathered[..., depth:], 1, size=rows).reshape(peers * rows, LANES)

    projected, packed = pack(codes.astype(F32), terms, experts, capacity)
    packed = lax.all_to_all(packed, BLOCKS, split_axis=0, concat_axis=0, tiled=True)
    packed = packed.reshape(2, 2, peers // 2, 2, capacity, peers, piece_width)
    piece = jnp.transpose(packed, (1, 4, 5, 0, 3, 2, 6)).reshape(capacity * blocks, features)

    pieces = gather_block(piece)
    pieces[-1], state_out = lax.optimization_barrier((pieces[-1], state_out))
    result = scatter_block(expert_ffn(pieces, gate, up, down))

    result = result.reshape(2, capacity, 2, peers // 2, features)
    result = jnp.transpose(result, (2, 0, 3, 1, 4)).reshape(blocks, capacity, features)
    mixed = projected.reshape(2, 1, peers // 2, capacity, 2 * width)
    mixed = jnp.broadcast_to(mixed, (2, 2) + mixed.shape[2:]).reshape(blocks, capacity, 2 * width)
    result = lax.all_to_all(
        jnp.concatenate([result, mixed], axis=2), BLOCKS, split_axis=0, concat_axis=0, tiled=True
    )
    mixed = result[..., features:].reshape(2, 2, peers // 2, rows, 2, piece_width)
    mixed = lax.dynamic_index_in_dim(mixed, lax.axis_index("yl"), 1, keepdims=False)
    mixed = jnp.transpose(mixed, (2, 0, 3, 1, 4)).reshape(rows, features)
    weights = jnp.sum(
        place(of_step(route_ids, 0)[0], experts, capacity) * of_step(route_gate, 0)[0], axis=-1
    )
    combined = jnp.einsum(
        "esr,esd->rd", weights, result[..., :features].astype(F32), precision=EXACT
    ).astype(BF16)
    both = spread(jnp.concatenate([mixed, combined], axis=0), "head")
    return both[:, :rows], both[:, rows:], state_out


def solution(mesh):
    shape = dict(mesh.shape)
    heads, peers = shape["head"], shape["expert"]
    split = (2, 2, peers // 16, 2, 2)
    fine = Mesh(mesh.devices.reshape((heads,) + split), ("head",) + EXPERT)
    return jax.shard_map(
        shards,
        mesh=fine,
        in_specs=(
            P(None, EXPERT, "head"),
            P(None, EXPERT, "head"),
            P(None, EXPERT, "head"),
            P("head"),
            P(EXPERT, "head", None, None),
            P("head", EXPERT),
            P(None, EXPERT, None),
            P(None, EXPERT, None),
            P(EXPERT, None, "head"),
            P(EXPERT, None, "head"),
            P(EXPERT, "head", None),
        ),
        out_specs=(
            P(None, EXPERT, None),
            P(None, EXPERT, None),
            P(EXPERT, "head", None, None),
        ),
        check_vma=False,
    )
```

```python
import functools

import jax
import jax.numpy as jnp
from jax import lax
from jax.experimental import pallas as pl
from jax.experimental.pallas import tpu as pltpu
from jax.sharding import Mesh, PartitionSpec as P

BLOCKS = ("yh", "yl", "zp")
PEERS = ("yh", "zp")
EXPERT = BLOCKS + ("zl", "core")
BF16 = jnp.bfloat16
F32 = jnp.float32
LANES = 128
EXACT = lax.Precision.HIGHEST


def shift(array, axis, distance):
    size = lax.axis_size(axis)
    pairs = [(i, (i + distance) % size) for i in range(size)]
    return lax.ppermute(array, axis, pairs)


def spread(array, axis):
    size = lax.axis_size(axis)
    copies = jnp.broadcast_to(array[None], (size,) + array.shape)
    return lax.all_to_all(copies, axis, split_axis=0, concat_axis=0, tiled=True)


def split(array):
    high = array.astype(BF16)
    return high, (array - high.astype(F32)).astype(BF16)


def attend_kernel(capacity, forget_ref, ids_ref, *refs):
    sources, out_ref, flat, landed, arrived = refs[:4], refs[4], refs[5], refs[6:10], refs[10]
    copies = [
        pltpu.make_async_copy(source, target, arrived.at[i])
        for i, (source, target) in enumerate(zip(sources, landed))
    ]
    for copy in copies:
        copy.start()
    query_ref, key_ref, value_ref, state_ref = landed
    steps, rows, width = query_ref.shape
    heads, size = state_ref.shape[1], state_ref.shape[2]
    count = steps * rows
    shape = (count, LANES)
    row, lane = (lax.broadcasted_iota(jnp.int32, shape, i) for i in range(2))
    tail = jnp.zeros(shape, jnp.int32)
    for t in range(steps):
        ids = [ids_ref[t, i // 2, i % 2] for i in range(2 * rows)]
        for i in range(2 * rows):
            slot = sum((jnp.where(ids[j] == ids[i], 1, 0) for j in range(i)), jnp.int32(0))
            here = (row == t * rows + i // 2) & (lane == i % 2)
            tail = jnp.where(here, ids[i] * capacity + slot, tail)
    tail = tail.astype(F32).astype(BF16)
    for copy in copies:
        copy.wait()
    for i, ref in enumerate((query_ref, key_ref, value_ref)):
        for t in range(steps):
            flat[i, t * rows : (t + 1) * rows] = ref[t].astype(F32)
    row_of = lax.broadcasted_iota(jnp.int32, (count, 1), 0)
    age = (row_of // rows + 1).astype(F32)
    member = row_of % rows
    one = lax.broadcasted_iota(jnp.int32, (count, count), 0)
    other = lax.broadcasted_iota(jnp.int32, (count, count), 1)
    lag = one // rows - other // rows
    seen = (lag >= 0) & (one % rows == other % rows)
    gap = jnp.maximum(lag, 0).astype(F32)
    for h in range(heads):
        lanes = slice(h * size, (h + 1) * size)
        rate = forget_ref[h]
        query, key, value = (flat[i, :, lanes].astype(BF16) for i in range(3))
        from_state = jnp.zeros((count, size), F32)
        for r in range(rows):
            product = jnp.dot(query, state_ref[r, h], preferred_element_type=F32)
            from_state += jnp.where(member == r, product, 0.0)
        scores = across_lanes(query, key) * jnp.where(seen, jnp.exp(-rate * gap), 0.0)
        from_steps = sum(jnp.dot(s, value, preferred_element_type=F32) for s in split(scores))
        attended = (jnp.exp(-rate * age) * from_state + from_steps).astype(BF16)
        for i in range(out_ref.shape[0]):
            out_ref[i, :, lanes] = attended
    for i in range(out_ref.shape[0]):
        out_ref[i, :, width:] = tail


def attend(query_rows, key_rows, value_rows, forget, head_state, route_ids, capacity, copies):
    steps, rows, width = query_rows.shape
    count = steps * rows
    whole = pl.BlockSpec(memory_space=pltpu.VMEM)
    return pl.pallas_call(
        functools.partial(attend_kernel, capacity),
        in_specs=[pl.BlockSpec(memory_space=pltpu.SMEM)] * 2
        + [pl.BlockSpec(memory_space=pltpu.HBM)] * 4,
        out_specs=whole,
        out_shape=jax.ShapeDtypeStruct((copies, count, width + LANES), BF16),
        scratch_shapes=[pltpu.VMEM((3, count, width), F32)]
        + [pltpu.VMEM(query_rows.shape, BF16)] * 3
        + [pltpu.VMEM(head_state.shape, BF16), pltpu.SemaphoreType.DMA((4,))],
        compiler_params=pltpu.CompilerParams(vmem_limit_bytes=54 * 1024 * 1024),
    )(forget, route_ids, query_rows, key_rows, value_rows, head_state)


def state_kernel(forget_ref, key_ref, value_ref, state_ref, out_ref, flat):
    steps, rows, width = key_ref.shape
    heads, size = state_ref.shape[1], state_ref.shape[2]
    count = steps * rows
    for i, ref in enumerate((key_ref, value_ref)):
        for t in range(steps):
            flat[i, t * rows : (t + 1) * rows] = ref[t].astype(F32)
    row_of = lax.broadcasted_iota(jnp.int32, (count, 1), 0)
    left = (steps - 1 - row_of // rows).astype(F32)
    member = row_of % rows
    for h in range(heads):
        lanes = slice(h * size, (h + 1) * size)
        rate = forget_ref[h]
        decay = jnp.exp(-rate * jnp.full((1, 1), steps, F32))
        scaled = flat[0, :, lanes] * jnp.exp(-rate * left)
        value = flat[1, :, lanes].astype(BF16)
        values = jnp.concatenate([value, value], axis=0)
        for r in range(rows):
            terms = jnp.concatenate(split(jnp.where(member == r, scaled, 0.0)), axis=0)
            added = lax.dot_general(
                terms, values, (((0,), (0,)), ((), ())), preferred_element_type=F32
            )
            out_ref[r, h] = (decay * state_ref[r, h].astype(F32) + added).astype(BF16)


def last_state(key_rows, value_rows, forget, head_state):
    steps, rows, width = key_rows.shape
    whole = pl.BlockSpec(memory_space=pltpu.VMEM)
    return pl.pallas_call(
        state_kernel,
        in_specs=[pl.BlockSpec(memory_space=pltpu.SMEM)] + [whole] * 3,
        out_specs=whole,
        out_shape=jax.ShapeDtypeStruct(head_state.shape, BF16),
        scratch_shapes=[pltpu.VMEM((2, steps * rows, width), F32)],
        compiler_params=pltpu.CompilerParams(vmem_limit_bytes=12 * 1024 * 1024),
        cost_estimate=pl.CostEstimate(
            flops=4 * steps * rows * head_state.size,
            bytes_accessed=4 * head_state.size,
            transcendentals=0,
        ),
    )(forget, key_rows, value_rows, head_state)


def place(ids, experts, capacity):
    rows = ids.shape[-2]
    flat = ids.reshape(ids.shape[:-2] + (rows * 2,))
    onehot = (flat[..., None] == jnp.arange(experts, dtype=jnp.int32)).astype(jnp.int32)
    ranked = jnp.cumsum(onehot, axis=-2) - 1
    landed = onehot[..., None] * (
        ranked[..., None] == jnp.arange(capacity, dtype=jnp.int32)
    ).astype(jnp.int32)
    landed = jnp.moveaxis(landed, (-2, -1), (0, 1)).astype(F32)
    return landed.reshape(landed.shape[:-1] + (rows, 2))


def gather_block(own):
    half = own.shape[0] // 2
    left, right, across = shift(own, "head", 1), shift(own, "head", -1), shift(own, "zl", 1)

    def halves(one, other):
        return jnp.concatenate([one, other], axis=0)

    by_left = shift(halves(left[:half], across[:half]), "head", 1)
    by_right = shift(halves(right[half:], across[half:]), "head", -1)
    by_across = shift(halves(left[half:], right[:half]), "zl", 1)
    last_left = shift(by_left[half:], "head", 1)
    last_right = shift(by_right[half:], "head", -1)
    return [own, left, right, across, by_left, by_right, by_across, last_left, last_right]


def scatter_block(parts):
    own, left, right, across, by_left, by_right, by_across, last_left, last_right = parts
    half = own.shape[0] // 2

    def add(*terms):
        return sum(t.astype(F32) for t in terms).astype(BF16)

    def halves(one, other):
        return jnp.concatenate([one, other], axis=0)

    from_right = shift(last_left, "head", -1)
    from_left = shift(last_right, "head", 1)
    by_left = halves(by_left[:half], add(by_left[half:], from_right))
    by_right = halves(by_right[:half], add(by_right[half:], from_left))
    from_right = shift(by_left, "head", -1)
    from_left = shift(by_right, "head", 1)
    from_across = shift(by_across, "zl", 1)
    left = add(left, halves(from_right[:half], from_across[:half]))
    right = add(right, halves(from_across[half:], from_left[:half]))
    across = add(across, halves(from_right[half:], from_left[half:]))
    return add(own, shift(left, "head", -1), shift(right, "head", 1), shift(across, "zl", 1))


def across_lanes(one, other):
    return lax.dot_general(one, other, (((1,), (1,)), ((), ())), preferred_element_type=F32)


def ffn_kernel(count, tile, *refs):
    rows, refs = refs[:count], refs[count:]
    wide, down, refs = refs[:4], refs[4:6], refs[6:]
    outs, (sums, hidden) = refs[:count], refs[count:]
    width, features = down[0].shape

    def first(step, carry):
        lanes = pl.ds(pl.multiple_of(step * tile, tile), tile)
        block = jnp.concatenate([r[:, lanes] for r in rows], axis=0).T
        for i, w in enumerate(wide):
            here = slice(i * width, (i + 1) * width)
            product = jnp.dot(w[:, lanes], block, preferred_element_type=F32)
            sums[here] = jnp.where(step == 0, 0.0, sums[here]) + product
        return carry

    lax.fori_loop(0, features // tile, first, 0)
    value = sums[...]
    gated, lifted = value[: 2 * width], value[2 * width :]
    hidden[...] = (gated / (1.0 + jnp.exp(-gated)) * lifted).T.astype(BF16)

    def second(step, carry):
        lanes = pl.ds(pl.multiple_of(step * tile, tile), tile)
        weights = jnp.concatenate([w[:, lanes] for w in down], axis=0)
        total = jnp.dot(hidden[...], weights, preferred_element_type=F32).astype(BF16)
        start = 0
        for out in outs:
            out[:, lanes] = total[start : start + out.shape[0]]
            start += out.shape[0]
        return carry

    lax.fori_loop(0, features // tile, second, 0)


def expert_ffn(parts, gate, up, down):
    width, features = gate[0].shape
    total_rows = sum(p.shape[0] for p in parts)
    tile = min(features, 2048)
    weights = [pltpu.with_memory_space_constraint(w, pltpu.VMEM) for w in gate + up + down]
    whole = pl.BlockSpec(memory_space=pltpu.VMEM)
    return pl.pallas_call(
        functools.partial(ffn_kernel, len(parts), tile),
        in_specs=[whole] * (len(parts) + 6),
        out_specs=[whole] * len(parts),
        out_shape=[jax.ShapeDtypeStruct(p.shape, BF16) for p in parts],
        scratch_shapes=[
            pltpu.VMEM((4 * width, total_rows), F32),
            pltpu.VMEM((total_rows, 2 * width), BF16),
        ],
        compiler_params=pltpu.CompilerParams(vmem_limit_bytes=16 * 1024 * 1024),
        cost_estimate=pl.CostEstimate(
            flops=12 * total_rows * features * width,
            bytes_accessed=4 * total_rows * features,
            transcendentals=2 * total_rows * width,
        ),
    )(*parts, *weights)


def peer_columns(columns, payload):
    here, depth = columns.shape
    yl, zl, core = (lax.axis_index(axis) == 0 for axis in ("yl", "zl", "core"))
    by_zl, by_yl = shift(columns, "zl", 1), shift(columns, "yl", 1)
    by_both = lax.ppermute(columns, ("yl", "zl"), [(i, 3 - i) for i in range(4)])

    def ordered(first, own, other):
        return jnp.where(first, own, other), jnp.where(first, other, own)

    low, high = ordered(zl, columns, by_zl), ordered(zl, by_yl, by_both)
    first, second = ordered(yl, low[0], high[0]), ordered(yl, low[1], high[1])
    quad = jnp.stack([first[0], second[0], first[1], second[1]])
    quad, _ = lax.optimization_barrier((quad, payload))
    whole = jnp.stack(ordered(core, quad, shift(quad, "core", 1)), axis=1)
    return jnp.pad(whole.reshape(8 * here, depth), ((0, 0), (0, LANES)))


def pack_kernel(code_ref, *refs):
    terms, (sum_ref, out_ref, flat) = refs[:-3], refs[-3:]
    peers, rows, width = terms[0].shape
    experts, halves, places, half = out_ref.shape
    for p in range(peers):
        flat[p * rows : (p + 1) * rows] = sum(term[p] for term in terms)
    total = flat[...].astype(BF16)
    sum_ref[...] = total
    shape = (peers * rows, experts * places)
    lane = lax.broadcasted_iota(jnp.int32, shape, 1)
    peer = lax.broadcasted_iota(jnp.int32, shape, 0) // rows
    slot = (lane // peers).astype(F32)
    hit = (slot == code_ref[:, 0:1]) | (slot == code_ref[:, 1:2])
    route = jnp.where(hit & (lane % peers == peer), 1.0, 0.0).astype(BF16)
    packed = lax.dot_general(
        route, total, (((0,), (0,)), ((), ())), preferred_element_type=F32
    ).astype(BF16)
    for e in range(experts):
        for i in range(halves):
            out_ref[e, i] = packed[e * places : (e + 1) * places, i * half : (i + 1) * half]


def pack(codes, terms, experts, capacity):
    peers, rows, width = terms[0].shape
    whole = pl.BlockSpec(memory_space=pltpu.VMEM)
    return pl.pallas_call(
        pack_kernel,
        in_specs=[whole] * (1 + len(terms)),
        out_specs=[whole] * 2,
        out_shape=[
            jax.ShapeDtypeStruct((peers * rows, width), BF16),
            jax.ShapeDtypeStruct((experts, 2, capacity * peers, width // 2), BF16),
        ],
        scratch_shapes=[pltpu.VMEM((peers * rows, width), F32)],
        compiler_params=pltpu.CompilerParams(vmem_limit_bytes=8 * 1024 * 1024),
    )(codes, *terms)


def shards(
    query_rows,
    key_rows,
    value_rows,
    forget,
    head_state,
    out_weight,
    route_ids,
    route_gate,
    gate_weight,
    up_weight,
    down_weight,
):
    steps, rows, depth = query_rows.shape
    peers = lax.axis_size("yh") * lax.axis_size("zp")
    blocks = 2 * peers
    experts = blocks
    capacity = rows // 2
    head = lax.axis_index("head")

    payload = attend(
        query_rows, key_rows, value_rows, forget, head_state, route_ids, capacity, peers
    )
    state_out = last_state(key_rows, value_rows, forget, head_state)
    columns = peer_columns(out_weight.T, payload)
    width = columns.shape[0]
    piece_width = width // 2
    features = width * peers
    gathered = lax.all_to_all(payload, PEERS, split_axis=0, concat_axis=0, tiled=True)

    partial = lax.dot_general(
        gathered.reshape(peers * steps * rows, depth + LANES),
        columns,
        (((1,), (1,)), ((), ())),
        preferred_element_type=F32,
    ).reshape(peers, steps * rows, width)
    partial = lax.optimization_barrier(partial)

    def of_step(array, axis, there=head, size=1):
        return lax.dynamic_slice_in_dim(array, there * size, size, axis)

    terms = [of_step(partial, 1, size=rows)]
    for distance in range(1, steps):
        there = lax.rem(head + distance, steps)
        terms.append(shift(of_step(partial, 1, there, rows), "head", distance))
    codes = of_step(gathered[..., depth:], 1, size=rows).reshape(peers * rows, LANES)

    projected, packed = pack(codes.astype(F32), terms, experts, capacity)
    own, packed = lax.optimization_barrier(
        ((gate_weight[0].T, up_weight[0].T, down_weight[0]), packed)
    )
    packed = lax.all_to_all(packed, BLOCKS, split_axis=0, concat_axis=0, tiled=True)
    other, packed = lax.optimization_barrier((tuple(shift(w, "core", 1) for w in own), packed))
    gate, up, down = zip(own, other)
    packed = packed.reshape(2, 2, peers // 2, 2, capacity, peers, piece_width)
    piece = jnp.transpose(packed, (1, 4, 5, 0, 3, 2, 6)).reshape(capacity * blocks, features)

    pieces = gather_block(piece)
    pieces[-1], state_out = lax.optimization_barrier((pieces[-1], state_out))
    result = scatter_block(expert_ffn(pieces, gate, up, down))

    result = result.reshape(2, capacity, 2, peers // 2, features)
    result = jnp.transpose(result, (2, 0, 3, 1, 4)).reshape(blocks, capacity, features)
    mixed = projected.reshape(2, 1, peers // 2, capacity, 2 * width)
    mixed = jnp.broadcast_to(mixed, (2, 2) + mixed.shape[2:]).reshape(blocks, capacity, 2 * width)
    result = lax.all_to_all(
        jnp.concatenate([result, mixed], axis=2), BLOCKS, split_axis=0, concat_axis=0, tiled=True
    )
    mixed = result[..., features:].reshape(2, 2, peers // 2, rows, 2, piece_width)
    mixed = lax.dynamic_index_in_dim(mixed, lax.axis_index("yl"), 1, keepdims=False)
    mixed = jnp.transpose(mixed, (2, 0, 3, 1, 4)).reshape(rows, features)
    weights = jnp.sum(
        place(of_step(route_ids, 0)[0], experts, capacity) * of_step(route_gate, 0)[0], axis=-1
    )
    combined = jnp.einsum(
        "esr,esd->rd", weights, result[..., :features].astype(F32), precision=EXACT
    ).astype(BF16)
    both = spread(jnp.concatenate([mixed, combined], axis=0), "head")
    return both[:, :rows], both[:, rows:], state_out


def solution(mesh):
    shape = dict(mesh.shape)
    heads, peers = shape["head"], shape["expert"]
    split = (2, 2, peers // 16, 2, 2)
    fine = Mesh(mesh.devices.reshape((heads,) + split), ("head",) + EXPERT)
    return jax.shard_map(
        shards,
        mesh=fine,
        in_specs=(
            P(None, EXPERT, "head"),
            P(None, EXPERT, "head"),
            P(None, EXPERT, "head"),
            P("head"),
            P(EXPERT, "head", None, None),
            P("head", EXPERT),
            P(None, EXPERT, None),
            P(None, EXPERT, None),
            P(EXPERT, None, "head"),
            P(EXPERT, None, "head"),
            P(EXPERT, "head", None),
        ),
        out_specs=(
            P(None, EXPERT, None),
            P(None, EXPERT, None),
            P(EXPERT, "head", None, None),
        ),
        check_vma=False,
    )
```

```python
import functools

import jax
import jax.numpy as jnp
from jax import lax
from jax.experimental import pallas as pl
from jax.experimental.pallas import tpu as pltpu
from jax.sharding import Mesh, PartitionSpec as P

BLOCKS = ("yh", "yl", "zp")
PEERS = ("yh", "zp")
EXPERT = BLOCKS + ("zl", "core")
BF16 = jnp.bfloat16
F32 = jnp.float32
LANES = 128
EXACT = lax.Precision.HIGHEST


def shift(array, axis, distance):
    size = lax.axis_size(axis)
    pairs = [(i, (i + distance) % size) for i in range(size)]
    return lax.ppermute(array, axis, pairs)


def spread(array, axis):
    size = lax.axis_size(axis)
    copies = jnp.broadcast_to(array[None], (size,) + array.shape)
    return lax.all_to_all(copies, axis, split_axis=0, concat_axis=0, tiled=True)


def split(array):
    high = array.astype(BF16)
    return high, (array - high.astype(F32)).astype(BF16)


def attend_kernel(capacity, forget_ref, ids_ref, *refs):
    sources, out_ref, flat, landed, arrived = refs[:4], refs[4], refs[5], refs[6:10], refs[10]
    copies = [
        pltpu.make_async_copy(source, target, arrived.at[i])
        for i, (source, target) in enumerate(zip(sources, landed))
    ]
    for copy in copies:
        copy.start()
    query_ref, key_ref, value_ref, state_ref = landed
    steps, rows, width = query_ref.shape
    heads, size = state_ref.shape[1], state_ref.shape[2]
    count = steps * rows
    shape = (count, LANES)
    row, lane = (lax.broadcasted_iota(jnp.int32, shape, i) for i in range(2))
    tail = jnp.zeros(shape, jnp.int32)
    for t in range(steps):
        ids = [ids_ref[t, i % 2, i // 2] for i in range(2 * rows)]
        for i in range(2 * rows):
            slot = sum((jnp.where(ids[j] == ids[i], 1, 0) for j in range(i)), jnp.int32(0))
            here = (row == t * rows + i // 2) & (lane == i % 2)
            tail = jnp.where(here, ids[i] * capacity + slot, tail)
    tail = tail.astype(F32).astype(BF16)
    for copy in copies:
        copy.wait()
    for i, ref in enumerate((query_ref, key_ref, value_ref)):
        for t in range(steps):
            flat[i, t * rows : (t + 1) * rows] = ref[t].astype(F32)
    row_of = lax.broadcasted_iota(jnp.int32, (count, 1), 0)
    age = (row_of // rows + 1).astype(F32)
    member = row_of % rows
    one = lax.broadcasted_iota(jnp.int32, (count, count), 0)
    other = lax.broadcasted_iota(jnp.int32, (count, count), 1)
    lag = one // rows - other // rows
    seen = (lag >= 0) & (one % rows == other % rows)
    gap = jnp.maximum(lag, 0).astype(F32)
    for h in range(heads):
        lanes = slice(h * size, (h + 1) * size)
        rate = forget_ref[h]
        query, key, value = (flat[i, :, lanes].astype(BF16) for i in range(3))
        from_state = jnp.zeros((count, size), F32)
        for r in range(rows):
            product = jnp.dot(query, state_ref[r, h], preferred_element_type=F32)
            from_state += jnp.where(member == r, product, 0.0)
        scores = across_lanes(query, key) * jnp.where(seen, jnp.exp(-rate * gap), 0.0)
        from_steps = sum(jnp.dot(s, value, preferred_element_type=F32) for s in split(scores))
        attended = (jnp.exp(-rate * age) * from_state + from_steps).astype(BF16)
        for i in range(out_ref.shape[0]):
            out_ref[i, :, lanes] = attended
    for i in range(out_ref.shape[0]):
        out_ref[i, :, width:] = tail


def attend(query_rows, key_rows, value_rows, forget, head_state, route_ids, capacity, copies):
    steps, rows, width = query_rows.shape
    count = steps * rows
    whole = pl.BlockSpec(memory_space=pltpu.VMEM)
    return pl.pallas_call(
        functools.partial(attend_kernel, capacity),
        in_specs=[pl.BlockSpec(memory_space=pltpu.SMEM)] * 2
        + [pl.BlockSpec(memory_space=pltpu.HBM)] * 4,
        out_specs=whole,
        out_shape=jax.ShapeDtypeStruct((copies, count, width + LANES), BF16),
        scratch_shapes=[pltpu.VMEM((3, count, width), F32)]
        + [pltpu.VMEM(query_rows.shape, BF16)] * 3
        + [pltpu.VMEM(head_state.shape, BF16), pltpu.SemaphoreType.DMA((4,))],
        compiler_params=pltpu.CompilerParams(vmem_limit_bytes=54 * 1024 * 1024),
    )(forget, jnp.swapaxes(route_ids, 1, 2), query_rows, key_rows, value_rows, head_state)


def state_kernel(forget_ref, key_ref, value_ref, state_ref, out_ref, flat):
    steps, rows, width = key_ref.shape
    heads, size = state_ref.shape[1], state_ref.shape[2]
    count = steps * rows
    for i, ref in enumerate((key_ref, value_ref)):
        for t in range(steps):
            flat[i, t * rows : (t + 1) * rows] = ref[t].astype(F32)
    row_of = lax.broadcasted_iota(jnp.int32, (count, 1), 0)
    left = (steps - 1 - row_of // rows).astype(F32)
    member = row_of % rows
    for h in range(heads):
        lanes = slice(h * size, (h + 1) * size)
        rate = forget_ref[h]
        decay = jnp.exp(-rate * jnp.full((1, 1), steps, F32))
        scaled = flat[0, :, lanes] * jnp.exp(-rate * left)
        value = flat[1, :, lanes].astype(BF16)
        values = jnp.concatenate([value, value], axis=0)
        for r in range(rows):
            terms = jnp.concatenate(split(jnp.where(member == r, scaled, 0.0)), axis=0)
            added = lax.dot_general(
                terms, values, (((0,), (0,)), ((), ())), preferred_element_type=F32
            )
            out_ref[r, h] = (decay * state_ref[r, h].astype(F32) + added).astype(BF16)


def last_state(key_rows, value_rows, forget, head_state):
    steps, rows, width = key_rows.shape
    whole = pl.BlockSpec(memory_space=pltpu.VMEM)
    return pl.pallas_call(
        state_kernel,
        in_specs=[pl.BlockSpec(memory_space=pltpu.SMEM)] + [whole] * 3,
        out_specs=whole,
        out_shape=jax.ShapeDtypeStruct(head_state.shape, BF16),
        scratch_shapes=[pltpu.VMEM((2, steps * rows, width), F32)],
        compiler_params=pltpu.CompilerParams(vmem_limit_bytes=12 * 1024 * 1024),
        cost_estimate=pl.CostEstimate(
            flops=4 * steps * rows * head_state.size,
            bytes_accessed=4 * head_state.size,
            transcendentals=0,
        ),
    )(forget, key_rows, value_rows, head_state)


def place(ids, experts, capacity):
    rows = ids.shape[-2]
    flat = ids.reshape(ids.shape[:-2] + (rows * 2,))
    onehot = (flat[..., None] == jnp.arange(experts, dtype=jnp.int32)).astype(jnp.int32)
    ranked = jnp.cumsum(onehot, axis=-2) - 1
    landed = onehot[..., None] * (
        ranked[..., None] == jnp.arange(capacity, dtype=jnp.int32)
    ).astype(jnp.int32)
    landed = jnp.moveaxis(landed, (-2, -1), (0, 1)).astype(F32)
    return landed.reshape(landed.shape[:-1] + (rows, 2))


def gather_block(own):
    half = own.shape[0] // 2
    across, left, right = shift(own, "zl", 1), shift(own, "head", 1), shift(own, "head", -1)

    def halves(one, other):
        return jnp.concatenate([one, other], axis=0)

    by_left = shift(halves(left[:half], across[:half]), "head", 1)
    by_right = shift(halves(right[half:], across[half:]), "head", -1)
    by_across = shift(halves(left[half:], right[:half]), "zl", 1)
    last_left = shift(by_left[half:], "head", 1)
    last_right = shift(by_right[half:], "head", -1)
    return [own, left, right, across, by_left, by_right, by_across, last_left, last_right]


def scatter_block(parts):
    own, left, right, across, by_left, by_right, by_across, last_left, last_right = parts
    half = own.shape[0] // 2

    def add(*terms):
        return sum(t.astype(F32) for t in terms).astype(BF16)

    def halves(one, other):
        return jnp.concatenate([one, other], axis=0)

    from_right = shift(last_left, "head", -1)
    from_left = shift(last_right, "head", 1)
    by_left = halves(by_left[:half], add(by_left[half:], from_right))
    by_right = halves(by_right[:half], add(by_right[half:], from_left))
    from_across = shift(by_across, "zl", 1)
    from_right = shift(by_left, "head", -1)
    from_left = shift(by_right, "head", 1)
    left = add(left, halves(from_right[:half], from_across[:half]))
    right = add(right, halves(from_across[half:], from_left[:half]))
    across = add(across, halves(from_right[half:], from_left[half:]))
    terms = shift(across, "zl", 1), shift(left, "head", -1), shift(right, "head", 1)
    return add(own, *terms)


def across_lanes(one, other):
    return lax.dot_general(one, other, (((1,), (1,)), ((), ())), preferred_element_type=F32)


def ffn_kernel(count, tile, *refs):
    rows, refs = refs[:count], refs[count:]
    wide, down, refs = refs[:4], refs[4:6], refs[6:]
    outs, (sums, hidden) = refs[:count], refs[count:]
    width, features = down[0].shape

    def first(step, carry):
        lanes = pl.ds(pl.multiple_of(step * tile, tile), tile)
        block = jnp.concatenate([r[:, lanes] for r in rows], axis=0).T
        for i, w in enumerate(wide):
            here = slice(i * width, (i + 1) * width)
            product = jnp.dot(w[:, lanes], block, preferred_element_type=F32)
            sums[here] = jnp.where(step == 0, 0.0, sums[here]) + product
        return carry

    lax.fori_loop(0, features // tile, first, 0)
    value = sums[...]
    gated, lifted = value[: 2 * width], value[2 * width :]
    hidden[...] = (gated / (1.0 + jnp.exp(-gated)) * lifted).T.astype(BF16)

    def second(step, carry):
        lanes = pl.ds(pl.multiple_of(step * tile, tile), tile)
        weights = jnp.concatenate([w[:, lanes] for w in down], axis=0)
        total = jnp.dot(hidden[...], weights, preferred_element_type=F32).astype(BF16)
        start = 0
        for out in outs:
            out[:, lanes] = total[start : start + out.shape[0]]
            start += out.shape[0]
        return carry

    lax.fori_loop(0, features // tile, second, 0)


def expert_ffn(parts, gate, up, down):
    width, features = gate[0].shape
    total_rows = sum(p.shape[0] for p in parts)
    tile = min(features, 2048)
    weights = [pltpu.with_memory_space_constraint(w, pltpu.VMEM) for w in gate + up + down]
    whole = pl.BlockSpec(memory_space=pltpu.VMEM)
    return pl.pallas_call(
        functools.partial(ffn_kernel, len(parts), tile),
        in_specs=[whole] * (len(parts) + 6),
        out_specs=[whole] * len(parts),
        out_shape=[jax.ShapeDtypeStruct(p.shape, BF16) for p in parts],
        scratch_shapes=[
            pltpu.VMEM((4 * width, total_rows), F32),
            pltpu.VMEM((total_rows, 2 * width), BF16),
        ],
        compiler_params=pltpu.CompilerParams(vmem_limit_bytes=16 * 1024 * 1024),
        cost_estimate=pl.CostEstimate(
            flops=12 * total_rows * features * width,
            bytes_accessed=4 * total_rows * features,
            transcendentals=2 * total_rows * width,
        ),
    )(*parts, *weights)


def peer_columns(columns, payload):
    here, depth = columns.shape
    yl, zl, core = (lax.axis_index(axis) == 0 for axis in ("yl", "zl", "core"))
    by_zl, by_yl = shift(columns, "zl", 1), shift(columns, "yl", 1)
    by_both = lax.ppermute(columns, ("yl", "zl"), [(i, 3 - i) for i in range(4)])

    def ordered(first, own, other):
        return jnp.where(first, own, other), jnp.where(first, other, own)

    low, high = ordered(zl, columns, by_zl), ordered(zl, by_yl, by_both)
    first, second = ordered(yl, low[0], high[0]), ordered(yl, low[1], high[1])
    quad = jnp.stack([first[0], second[0], first[1], second[1]])
    quad, _ = lax.optimization_barrier((quad, payload))
    whole = jnp.stack(ordered(core, quad, shift(quad, "core", 1)), axis=1)
    return jnp.pad(whole.reshape(8 * here, depth), ((0, 0), (0, LANES)))


def pack_kernel(code_ref, *refs):
    terms, (sum_ref, out_ref, flat) = refs[:-3], refs[-3:]
    peers, rows, width = terms[0].shape
    experts, halves, places, half = out_ref.shape
    for p in range(peers):
        flat[p * rows : (p + 1) * rows] = sum(term[p] for term in terms)
    total = flat[...].astype(BF16)
    sum_ref[...] = total
    shape = (peers * rows, experts * places)
    lane = lax.broadcasted_iota(jnp.int32, shape, 1)
    peer = lax.broadcasted_iota(jnp.int32, shape, 0) // rows
    slot = (lane // peers).astype(F32)
    hit = (slot == code_ref[:, 0:1]) | (slot == code_ref[:, 1:2])
    route = jnp.where(hit & (lane % peers == peer), 1.0, 0.0).astype(BF16)
    packed = lax.dot_general(
        route, total, (((0,), (0,)), ((), ())), preferred_element_type=F32
    ).astype(BF16)
    for e in range(experts):
        for i in range(halves):
            out_ref[e, i] = packed[e * places : (e + 1) * places, i * half : (i + 1) * half]


def pack(codes, terms, experts, capacity):
    peers, rows, width = terms[0].shape
    whole = pl.BlockSpec(memory_space=pltpu.VMEM)
    return pl.pallas_call(
        pack_kernel,
        in_specs=[whole] * (1 + len(terms)),
        out_specs=[whole] * 2,
        out_shape=[
            jax.ShapeDtypeStruct((peers * rows, width), BF16),
            jax.ShapeDtypeStruct((experts, 2, capacity * peers, width // 2), BF16),
        ],
        scratch_shapes=[pltpu.VMEM((peers * rows, width), F32)],
        compiler_params=pltpu.CompilerParams(vmem_limit_bytes=8 * 1024 * 1024),
    )(codes, *terms)


def shards(
    query_rows,
    key_rows,
    value_rows,
    forget,
    head_state,
    out_weight,
    route_ids,
    route_gate,
    gate_weight,
    up_weight,
    down_weight,
):
    steps, rows, depth = query_rows.shape
    peers = lax.axis_size("yh") * lax.axis_size("zp")
    blocks = 2 * peers
    experts = blocks
    capacity = rows // 2
    head = lax.axis_index("head")

    payload = attend(
        query_rows, key_rows, value_rows, forget, head_state, route_ids, capacity, peers
    )
    state_out = last_state(key_rows, value_rows, forget, head_state)
    columns = peer_columns(out_weight.T, payload)
    width = columns.shape[0]
    piece_width = width // 2
    features = width * peers
    gathered = lax.all_to_all(payload, PEERS, split_axis=0, concat_axis=0, tiled=True)

    partial = lax.dot_general(
        gathered.reshape(peers * steps * rows, depth + LANES),
        columns,
        (((1,), (1,)), ((), ())),
        preferred_element_type=F32,
    ).reshape(peers, steps * rows, width)
    partial = lax.optimization_barrier(partial)

    def of_step(array, axis, there=head, size=1):
        return lax.dynamic_slice_in_dim(array, there * size, size, axis)

    terms = [of_step(partial, 1, size=rows)]
    for distance in range(1, steps):
        there = lax.rem(head + distance, steps)
        terms.append(shift(of_step(partial, 1, there, rows), "head", distance))
    codes = of_step(gathered[..., depth:], 1, size=rows).reshape(peers * rows, LANES)

    projected, packed = pack(codes.astype(F32), terms, experts, capacity)
    own, packed = lax.optimization_barrier(
        ((gate_weight[0].T, up_weight[0].T, down_weight[0]), packed)
    )
    packed = lax.all_to_all(packed, BLOCKS, split_axis=0, concat_axis=0, tiled=True)
    other, packed = lax.optimization_barrier((tuple(shift(w, "core", 1) for w in own), packed))
    gate, up, down = zip(own, other)
    packed = packed.reshape(2, 2, peers // 2, 2, capacity, peers, piece_width)
    piece = jnp.transpose(packed, (1, 4, 5, 0, 3, 2, 6)).reshape(capacity * blocks, features)

    pieces = gather_block(piece)
    pieces[-1], state_out = lax.optimization_barrier((pieces[-1], state_out))
    result = scatter_block(expert_ffn(pieces, gate, up, down))

    result = result.reshape(2, capacity, 2, peers // 2, features)
    result = jnp.transpose(result, (2, 0, 3, 1, 4)).reshape(blocks, capacity, features)
    mixed = projected.reshape(2, 1, peers // 2, capacity, 2 * width)
    mixed = jnp.broadcast_to(mixed, (2, 2) + mixed.shape[2:]).reshape(blocks, capacity, 2 * width)
    result = lax.all_to_all(
        jnp.concatenate([result, mixed], axis=2), BLOCKS, split_axis=0, concat_axis=0, tiled=True
    )
    mixed = result[..., features:].reshape(2, 2, peers // 2, rows, 2, piece_width)
    mixed = lax.dynamic_index_in_dim(mixed, lax.axis_index("yl"), 1, keepdims=False)
    mixed = jnp.transpose(mixed, (2, 0, 3, 1, 4)).reshape(rows, features)
    weights = jnp.sum(
        place(of_step(route_ids, 0)[0], experts, capacity) * of_step(route_gate, 0)[0], axis=-1
    )
    combined = jnp.einsum(
        "esr,esd->rd", weights, result[..., :features].astype(F32), precision=EXACT
    ).astype(BF16)
    both = spread(jnp.concatenate([mixed, combined], axis=0), "head")
    return both[:, :rows], both[:, rows:], state_out


def solution(mesh):
    shape = dict(mesh.shape)
    heads, peers = shape["head"], shape["expert"]
    split = (2, 2, peers // 16, 2, 2)
    fine = Mesh(mesh.devices.reshape((heads,) + split), ("head",) + EXPERT)
    return jax.shard_map(
        shards,
        mesh=fine,
        in_specs=(
            P(None, EXPERT, "head"),
            P(None, EXPERT, "head"),
            P(None, EXPERT, "head"),
            P("head"),
            P(EXPERT, "head", None, None),
            P("head", EXPERT),
            P(None, EXPERT, None),
            P(None, EXPERT, None),
            P(EXPERT, None, "head"),
            P(EXPERT, None, "head"),
            P(EXPERT, "head", None),
        ),
        out_specs=(
            P(None, EXPERT, None),
            P(None, EXPERT, None),
            P(EXPERT, "head", None, None),
        ),
        check_vma=False,
    )
```
